256 devices in a mesh: grp: 4 (over x), dev: 64 (over z, y, core).
Axes of the slice: x: 4, y: 4, z: 8, core: 2. Of those that a mesh axis runs over, the one named last changes fastest.
Arguments:
- filt_mean: float32 [512, 256], P(('grp', 'dev')), may hold values from -6 to 6
- filt_cov: float32 [512, 256, 256], P(('grp', 'dev')), may hold values from -6 to 10, as said below
- noise_cov: float32 [512, 256, 256], P(('grp', 'dev')), may hold values from -1.25 to 1.25, as said below
- transition: float32 [256, 256], replicated, may hold values from -1 to 1
Outputs:
- smooth_mean: float32 [512, 256], P(('grp', 'dev'))
- smooth_cov: float32 [512, 256, 256], P(('grp', 'dev'))
The draws below stay inside these ranges and needn't reach their ends.
Inputs may be any that keep to these rules, and one draw needn't show every extreme that they name: Each filt_cov[t] is symmetric positive definite. Each noise_cov[t] is symmetric positive definite.
All inputs are finite; a program needn't handle non-finite values.
Results may differ from the reference program's by a relative error of at most 0.0003.
Values sent between devices are 32-bit elements; how exact they have to be, the bound alone decides.
No kernel may reach another device: no remote copies, remote signals or barrier semaphores. Data moves between devices by JAX's collectives and lax.ppermute only.
A program may use at most 256 MiB of HBM per device.

```python
import math
import jax
import jax.numpy as jnp
from jax import lax

NS = 256
HORIZON_LENGTH = 512


def modal_basis(key):
    highest = lax.Precision.HIGHEST
    raw = jax.random.normal(jax.random.fold_in(key, 7), (NS, NS), jnp.float32)
    unit_matrix = jnp.eye(NS, dtype=jnp.float32)
    initial = 0.5 * (unit_matrix + 0.5 * raw / math.sqrt(NS))

    def refine(index_now, basis):
        square = jnp.matmul(basis, basis.T, precision=highest)
        return 1.5 * basis - 0.5 * jnp.matmul(square, basis, precision=highest)
    return lax.fori_loop(0, 40, refine, initial)


def draw_transition(key, part):
    highest = lax.Precision.HIGHEST
    basis = modal_basis(key)
    angles = jax.random.uniform(jax.random.fold_in(key, 8), (NS // 2,), jnp.float32, -math.pi, math.pi)
    per_state = jnp.repeat(angles, 2)
    rows = lax.broadcasted_iota(jnp.int32, (NS, NS), 0)
    cols = lax.broadcasted_iota(jnp.int32, (NS, NS), 1)
    cosine = jnp.cos(per_state)[:, None]
    sine = jnp.sin(per_state)[:, None]
    even_row = rows % 2 == 0
    rotation = jnp.where(rows == cols, cosine, 0.0)
    rotation = rotation + jnp.where(even_row & (cols == rows + 1), -sine, 0.0)
    rotation = rotation + jnp.where(jnp.logical_not(even_row) & (cols == rows - 1), sine, 0.0)
    turned = jnp.matmul(basis, rotation, precision=highest)
    return jnp.matmul(turned, basis.T, precision=highest).astype(jnp.float32)


def draw_noise_cov(key, part):
    highest = lax.Precision.HIGHEST
    basis = modal_basis(key)
    slow_share = 0.5
    spread_low = 0.7
    spread_high = 1.4
    coordinate_couples = NS // 2
    sluggish_components = jax.random.uniform(jax.random.fold_in(key, 9), (coordinate_couples,), jnp.float32) < slow_share
    slow_rate = jnp.exp(jax.random.uniform(jax.random.fold_in(key, 10), (coordinate_couples,), jnp.float32, math.log(0.05), math.log(0.25))) / HORIZON_LENGTH
    fast_rate = jnp.exp(jax.random.uniform(jax.random.fold_in(key, 11), (coordinate_couples,), jnp.float32, math.log(0.03), math.log(0.15)))
    floor_amount = jnp.where(sluggish_components, slow_rate, fast_rate)
    damping_width = jnp.exp(jax.random.uniform(jax.random.fold_in(key, 12), (HORIZON_LENGTH, coordinate_couples), jnp.float32, math.log(spread_low), math.log(spread_high)))
    time_marks = jax.random.randint(jax.random.fold_in(key, 13), (3,), 0, HORIZON_LENGTH)
    time_step_index = lax.broadcasted_iota(jnp.int32, (HORIZON_LENGTH, 3), 0)
    impulse_start_moment = jnp.any(time_step_index == time_marks[None, :], axis=1)
    wind_impulse = jax.random.uniform(jax.random.fold_in(key, 14), (HORIZON_LENGTH, coordinate_couples), jnp.float32, 0.4, 1.2)
    damping_factors = jnp.where(impulse_start_moment[:, None] & sluggish_components[None, :], wind_impulse, floor_amount[None, :] * damping_width)
    per_state = jnp.repeat(damping_factors, 2, axis=1)
    scaled = basis[None, :, :] * per_state[:, None, :]
    return jnp.matmul(scaled, basis.T, precision=highest).astype(jnp.float32)


def draw_filt_cov(key, part):
    highest = lax.Precision.HIGHEST
    scale_low = 0.5
    scale_high = 2.0
    scales = jnp.exp(jax.random.uniform(jax.random.fold_in(key, 21), (HORIZON_LENGTH, NS), jnp.float32, math.log(scale_low), math.log(scale_high)))
    edge = math.sqrt(3.0)
    raw = jax.random.uniform(jax.random.fold_in(key, 22), (HORIZON_LENGTH, NS, NS), jnp.float32, -edge, edge)
    gram = jnp.matmul(raw, jnp.swapaxes(raw, 1, 2), precision=highest) / NS
    gram = 0.5 * (gram + jnp.swapaxes(gram, 1, 2))
    core = jnp.eye(NS, dtype=jnp.float32)[None, :, :] + 0.5 * gram
    root = jnp.sqrt(scales)
    return (root[:, :, None] * core * root[:, None, :]).astype(jnp.float32)


def block_levels(rng, dims, shards, low, largest):
    def one(dim, shards_of):
        draws = jax.random.uniform(jax.random.fold_in(jax.random.fold_in(rng, 6), dim), (shards_of,), jnp.float32, low / len(shards), largest / len(shards))
        return jnp.repeat(jnp.exp(draws), dims[dim] // shards_of).reshape((-1,) + (1,) * (len(dims) - dim - 1))

    factor_of = one(*shards[0])
    for cut in shards[1:]:
        factor_of = factor_of * one(*cut)
    return factor_of


def normal_values(own_key, shape, width, bound, shards=(), kind=jnp.bfloat16):
    level = block_levels(own_key, shape, shards, -0.22, 0.18) if shards else 1.0
    array = jax.random.normal(own_key, shape, jnp.float32) * width * level
    return jnp.minimum(jnp.maximum(array, -bound), bound).astype(kind)


def setup_inputs(seed: int = 0) -> dict:
    key_list = jax.random.split(jax.random.key(seed), 5)
    return {
        "filt_mean": normal_values(key_list[0], (HORIZON_LENGTH, NS), 1.0, 6.0, ((0, 256),), jnp.float32),
        "filt_cov": draw_filt_cov(jax.random.fold_in(key_list[4], 71), 0),
        "noise_cov": draw_noise_cov(jax.random.fold_in(key_list[4], 71), 0),
        "transition": draw_transition(jax.random.fold_in(key_list[4], 71), 0),
    }


def product(left, right):
    return jnp.matmul(left, right, precision=lax.Precision.HIGHEST)

def chol_solve(factor, rhs):
    middle = lax.linalg.triangular_solve(factor, rhs, left_side=True, lower=True)
    return lax.linalg.triangular_solve(factor, middle, left_side=True, lower=True, transpose_a=True)

def reference(filt_mean, filt_cov, noise_cov, transition):
    last_mean = filt_mean[-1]
    last_cov = filt_cov[-1]

    def backward(running, inputs):
        mean_next, cov_next = running
        mean_now, cov_now, noise_now = inputs
        moved = product(transition, cov_now)
        predicted = product(moved, transition.T) + noise_now
        factor = jnp.linalg.cholesky(predicted)
        solved = chol_solve(factor, moved)
        gain_now = solved.T
        offset = mean_now - product(gain_now, product(transition, mean_now))
        remainder = cov_now - product(gain_now, moved)
        mean_smooth = product(gain_now, mean_next) + offset
        cov_smooth = product(product(gain_now, cov_next), gain_now.T) + remainder
        return ((mean_smooth, cov_smooth), (mean_smooth, cov_smooth))
    _, (means, covs) = lax.scan(backward, (last_mean, last_cov), (filt_mean[:-1], filt_cov[:-1], noise_cov[:-1]), reverse=True)
    smooth_mean = jnp.concatenate([means, last_mean[None]], axis=0)
    smooth_cov = jnp.concatenate([covs, last_cov[None]], axis=0)
    return (smooth_mean, smooth_cov)
```

```python
import jax
import jax.numpy as jnp
from jax import lax
from jax.sharding import PartitionSpec as P

AXES = ("grp", "dev")
EXTRA = 8


def product(left, right):
    return jnp.matmul(left, right, precision=lax.Precision.HIGHEST)


def flipped(matrix):
    return jnp.swapaxes(matrix, -1, -2)


def chol_solve(factor, rhs):
    middle = lax.linalg.triangular_solve(factor, rhs, left_side=True, lower=True)
    return lax.linalg.triangular_solve(factor, middle, left_side=True, lower=True, transpose_a=True)


def grown(matrix, row):
    return jnp.concatenate([matrix, jnp.broadcast_to(row, (EXTRA, row.shape[-1]))], axis=0)


def applied(turned, held_next, held):
    width = turned.shape[0]
    first = product(held_next, turned)
    square = product(flipped(turned), first[:width]) + held[:width]
    return jnp.concatenate([square, first[width:] + held[width:]], axis=0)


def local(filt_mean, filt_cov, noise_cov, transition):
    width = filt_mean.shape[1]
    devices = lax.axis_size(AXES)
    chips = devices // 2
    place = lax.axis_index(AXES)
    core = place % 2
    moved = product(transition, filt_cov)
    predicted = product(moved, transition.T) + noise_cov
    factor = jnp.linalg.cholesky(predicted)
    solved = chol_solve(factor, moved)
    final = (place == devices - 1) & (jnp.arange(2) == 1)
    solved = jnp.where(final[:, None, None], 0.0, solved)
    ahead = product(filt_mean, transition.T)
    offset = filt_mean - product(ahead[:, None, :], solved)[:, 0]
    remainder = filt_cov - product(flipped(solved), moved)
    turned = [solved[0], solved[1]]
    held = [grown(remainder[0], offset[0]), grown(remainder[1], offset[1])]
    both_turned = product(turned[1], turned[0])
    both_held = applied(turned[0], held[1], held[0])
    swap = [(p, p ^ 1) for p in range(devices)]
    other_turned = lax.ppermute(both_turned, AXES, swap)
    other_held = lax.ppermute(both_held, AXES, swap)
    is_first = core == 0
    a_turned = jnp.where(is_first, both_turned, other_turned)
    b_turned = jnp.where(is_first, other_turned, both_turned)
    a_held = jnp.where(is_first, both_held, other_held)
    b_held = jnp.where(is_first, other_held, both_held)
    chip_turned = product(b_turned, a_turned)
    chip_held = applied(a_turned, b_held, a_held)
    late = [jnp.where(is_first, product(other_turned, t), t) for t in (both_turned, turned[1])]
    late_held = [
        jnp.where(is_first, applied(t, other_held, h), h)
        for t, h in ((both_turned, both_held), (turned[1], held[1]))
    ]
    blank = jnp.zeros((EXTRA, width), jnp.float32)
    mine = jnp.where(is_first, jnp.concatenate([chip_turned, blank], axis=0), chip_held)
    gain = chip_turned
    stride = 1
    while stride < chips:
        pairs = [(2 * (c + stride) + 1, 2 * c + 1) for c in range(chips - stride)]
        pairs += [(2 * (c + stride), 2 * c) for c in range(chips - 2 * stride)]
        got = lax.ppermute(mine, AXES, pairs)
        first = product(got, gain)
        if stride * 2 < chips:
            passed = lax.ppermute(first[:width], AXES, [(2 * c, 2 * c + 1) for c in range(chips)])
            later = jnp.where(is_first, first[:width], passed)
        square = product(flipped(gain), first[:width]) + mine[:width]
        row = first[width:] + mine[width:]
        mine = jnp.where(is_first, first, jnp.concatenate([square, row], axis=0))
        gain = later
        stride *= 2
    to_second = lax.ppermute(mine, AXES, [(2 * c + 3, 2 * c + 1) for c in range(chips - 1)])
    to_first = lax.ppermute(mine, AXES, [(2 * c + 3, 2 * c) for c in range(chips - 1)])
    after = jnp.where(is_first, to_first, to_second)
    outs = [applied(t, after, h) for t, h in zip(late, late_held)]
    smooth_cov = jnp.stack([o[:width] for o in outs])
    smooth_mean = jnp.stack([o[width] for o in outs])
    return (smooth_mean, smooth_cov)


def solution(mesh):
    in_specs = (P(AXES, None), P(AXES, None, None), P(AXES, None, None), P())
    out_specs = (P(AXES, None), P(AXES, None, None))
    return jax.shard_map(local, mesh=mesh, in_specs=in_specs, out_specs=out_specs, check_vma=False)
```

```python
import jax
import jax.numpy as jnp
from jax import lax
from jax.experimental import pallas as pl
from jax.experimental.pallas import tpu as pltpu
from jax.sharding import PartitionSpec as P

AXES = ("grp", "dev")
EXTRA = 8

BASE = 32
HALF = 128


def dot(left, right):
    return jnp.dot(left, right, precision=lax.Precision.HIGHEST, preferred_element_type=jnp.float32)


def base_inverse(first, second):
    unit = (lax.broadcasted_iota(jnp.int32, (BASE, BASE), 0) == lax.broadcasted_iota(jnp.int32, (BASE, BASE), 1)).astype(jnp.float32)
    whole = jnp.concatenate([first, unit, second, unit], axis=1)
    tiles = [whole[8 * i : 8 * i + 8] for i in range(BASE // 8)]
    lane = lax.broadcasted_iota(jnp.int32, (8, 128), 1)
    sub = lax.broadcasted_iota(jnp.int32, (8, 128), 0)
    for q in range(BASE // 8):
        cols = []
        for j in range(8):
            at = 8 * q + j
            cols.append([
                jnp.where(lane < 64, jnp.broadcast_to(t[:, at : at + 1], (8, 128)), jnp.broadcast_to(t[:, 64 + at : 65 + at], (8, 128)))
                for t in tiles
            ])
        for k in range(8):
            def row(t):
                return jnp.broadcast_to(t[k : k + 1], (8, 128))
            ratio = 1.0 / row(cols[k][q])
            scaled = row(tiles[q]) * ratio
            factors = [row(cols[j][q]) * ratio for j in range(k + 1, 8)]
            down = list(cols[k])
            down[q] = down[q] - jnp.where(sub == k, 1.0, 0.0)
            tiles = [t - d * scaled for t, d in zip(tiles, down)]
            for j, f in zip(range(k + 1, 8), factors):
                cols[j] = [c - d * f for c, d in zip(cols[j], down)]
    whole = jnp.concatenate(tiles, axis=0)
    return whole[:, BASE : 2 * BASE], whole[:, 64 + BASE : 64 + 2 * BASE]


def half_inverse(work):
    for j in range(HALF // BASE):
        rows = slice(BASE * j, BASE * j + BASE)
        inv = base_inverse(work[0, rows, rows], work[1, rows, rows])
        lane = lax.broadcasted_iota(jnp.int32, (HALF, HALF), 1)
        inside = (lane >= BASE * j) & (lane < BASE * (j + 1))
        r = lax.broadcasted_iota(jnp.int32, (BASE, HALF), 0)
        c = lax.broadcasted_iota(jnp.int32, (BASE, HALF), 1)
        for m in range(2):
            old = work[m]
            top = jnp.where(inside[:BASE], (c == r + BASE * j).astype(jnp.float32), old[rows])
            new = dot(inv[m], top)
            work[m] = jnp.where(inside, 0.0, old) - dot(old[:, rows], new)
            work[m, rows] = new


def solve_kernel(pred, moved, out, work):
    lo, hi = slice(0, HALF), slice(HALF, 2 * HALF)
    for m in range(2):
        work[m] = pred[m, lo, lo]
    half_inverse(work)
    wide, rest = [], []
    for m in range(2):
        rhs = jnp.concatenate([pred[m, lo, hi], moved[m, lo]], axis=1)
        w = dot(work[m], rhs)
        s = jnp.concatenate([pred[m, hi, hi], moved[m, hi]], axis=1) - dot(pred[m, hi, lo], w)
        wide.append(w)
        rest.append(s[:, HALF:])
        work[m] = s[:, :HALF]
    half_inverse(work)
    for m in range(2):
        h2 = dot(work[m], rest[m])
        out[m, hi] = h2
        out[m, lo] = wide[m][:, HALF:] - dot(wide[m][:, :HALF], h2)


def solve(pred, moved):
    return pl.pallas_call(
        solve_kernel,
        out_shape=jax.ShapeDtypeStruct(moved.shape, jnp.float32),
        in_specs=[pl.BlockSpec(memory_space=pltpu.VMEM)] * 2,
        out_specs=pl.BlockSpec(memory_space=pltpu.VMEM),
        scratch_shapes=[pltpu.VMEM((2, HALF, HALF), jnp.float32)],
        compiler_params=pltpu.CompilerParams(vmem_limit_bytes=32 * 1024 * 1024),
    )(pred, moved)


def product(left, right):
    return jnp.matmul(left, right, precision=lax.Precision.HIGHEST)


def flipped(matrix):
    return jnp.swapaxes(matrix, -1, -2)


def grown(matrix, row):
    return jnp.concatenate([matrix, jnp.broadcast_to(row, (EXTRA, row.shape[-1]))], axis=0)


def applied(turned, held_next, held):
    width = turned.shape[0]
    first = product(held_next, turned)
    square = product(flipped(turned), first[:width]) + held[:width]
    return jnp.concatenate([square, first[width:] + held[width:]], axis=0)


def local(filt_mean, filt_cov, noise_cov, transition):
    width = filt_mean.shape[1]
    devices = lax.axis_size(AXES)
    chips = devices // 2
    place = lax.axis_index(AXES)
    core = place % 2
    moved = product(transition, filt_cov)
    predicted = product(moved, transition.T) + noise_cov
    solved = solve(predicted, moved)
    final = (place == devices - 1) & (jnp.arange(2) == 1)
    solved = jnp.where(final[:, None, None], 0.0, solved)
    ahead = product(filt_mean, transition.T)
    offset = filt_mean - product(ahead[:, None, :], solved)[:, 0]
    remainder = filt_cov - product(flipped(solved), moved)
    turned = [solved[0], solved[1]]
    held = [grown(remainder[0], offset[0]), grown(remainder[1], offset[1])]
    both_turned = product(turned[1], turned[0])
    both_held = applied(turned[0], held[1], held[0])
    swap = [(p, p ^ 1) for p in range(devices)]
    other_turned = lax.ppermute(both_turned, AXES, swap)
    other_held = lax.ppermute(both_held, AXES, swap)
    is_first = core == 0
    a_turned = jnp.where(is_first, both_turned, other_turned)
    b_turned = jnp.where(is_first, other_turned, both_turned)
    a_held = jnp.where(is_first, both_held, other_held)
    b_held = jnp.where(is_first, other_held, both_held)
    chip_turned = product(b_turned, a_turned)
    chip_held = applied(a_turned, b_held, a_held)
    late = [jnp.where(is_first, product(other_turned, t), t) for t in (both_turned, turned[1])]
    late_held = [
        jnp.where(is_first, applied(t, other_held, h), h)
        for t, h in ((both_turned, both_held), (turned[1], held[1]))
    ]
    blank = jnp.zeros((EXTRA, width), jnp.float32)
    mine = jnp.where(is_first, jnp.concatenate([chip_turned, blank], axis=0), chip_held)
    gain = chip_turned
    stride = 1
    while stride < chips:
        pairs = [(2 * (c + stride) + 1, 2 * c + 1) for c in range(chips - stride)]
        pairs += [(2 * (c + stride), 2 * c) for c in range(chips - 2 * stride)]
        got = lax.ppermute(mine, AXES, pairs)
        first = product(got, gain)
        if stride * 2 < chips:
            passed = lax.ppermute(first[:width], AXES, [(2 * c, 2 * c + 1) for c in range(chips)])
            later = jnp.where(is_first, first[:width], passed)
        square = product(flipped(gain), first[:width]) + mine[:width]
        row = first[width:] + mine[width:]
        mine = jnp.where(is_first, first, jnp.concatenate([square, row], axis=0))
        gain = later
        stride *= 2
    to_second = lax.ppermute(mine, AXES, [(2 * c + 3, 2 * c + 1) for c in range(chips - 1)])
    to_first = lax.ppermute(mine, AXES, [(2 * c + 3, 2 * c) for c in range(chips - 1)])
    after = jnp.where(is_first, to_first, to_second)
    outs = [applied(t, after, h) for t, h in zip(late, late_held)]
    smooth_cov = jnp.stack([o[:width] for o in outs])
    smooth_mean = jnp.stack([o[width] for o in outs])
    return (smooth_mean, smooth_cov)


def solution(mesh):
    in_specs = (P(AXES, None), P(AXES, None, None), P(AXES, None, None), P())
    out_specs = (P(AXES, None), P(AXES, None, None))
    return jax.shard_map(local, mesh=mesh, in_specs=in_specs, out_specs=out_specs, check_vma=False)
```

```python
import jax
import jax.numpy as jnp
from jax import lax
from jax.experimental import pallas as pl
from jax.experimental.pallas import tpu as pltpu
from jax.sharding import PartitionSpec as P

AXES = ("grp", "dev")
EXTRA = 8

BASE = 32
HALF = 128


def dot(left, right):
    return jnp.dot(left, right, precision=lax.Precision.HIGHEST, preferred_element_type=jnp.float32)


def base_inverse(first, second):
    unit = (lax.broadcasted_iota(jnp.int32, (BASE, BASE), 0) == lax.broadcasted_iota(jnp.int32, (BASE, BASE), 1)).astype(jnp.float32)
    whole = jnp.concatenate([first, unit, second, unit], axis=1)
    tiles = [whole[8 * i : 8 * i + 8] for i in range(BASE // 8)]
    lane = lax.broadcasted_iota(jnp.int32, (8, 128), 1)
    sub = lax.broadcasted_iota(jnp.int32, (8, 128), 0)
    for q in range(BASE // 8):
        cols = []
        for j in range(8):
            at = 8 * q + j
            cols.append([
                jnp.where(lane < 64, jnp.broadcast_to(t[:, at : at + 1], (8, 128)), jnp.broadcast_to(t[:, 64 + at : 65 + at], (8, 128)))
                for t in tiles
            ])
        for k in range(8):
            def row(t):
                return jnp.broadcast_to(t[k : k + 1], (8, 128))
            ratio = 1.0 / row(cols[k][q])
            scaled = row(tiles[q]) * ratio
            factors = [row(cols[j][q]) * ratio for j in range(k + 1, 8)]
            down = list(cols[k])
            down[q] = down[q] - jnp.where(sub == k, 1.0, 0.0)
            tiles = [t - d * scaled for t, d in zip(tiles, down)]
            for j, f in zip(range(k + 1, 8), factors):
                cols[j] = [c - d * f for c, d in zip(cols[j], down)]
    whole = jnp.concatenate(tiles, axis=0)
    return whole[:, BASE : 2 * BASE], whole[:, 64 + BASE : 64 + 2 * BASE]


def half_inverse(work):
    for j in range(HALF // BASE):
        rows = slice(BASE * j, BASE * j + BASE)
        inv = base_inverse(work[0, rows, rows], work[1, rows, rows])
        lane = lax.broadcasted_iota(jnp.int32, (HALF, HALF), 1)
        inside = (lane >= BASE * j) & (lane < BASE * (j + 1))
        r = lax.broadcasted_iota(jnp.int32, (BASE, HALF), 0)
        c = lax.broadcasted_iota(jnp.int32, (BASE, HALF), 1)
        for m in range(2):
            old = work[m]
            top = jnp.where(inside[:BASE], (c == r + BASE * j).astype(jnp.float32), old[rows])
            new = dot(inv[m], top)
            work[m] = jnp.where(inside, 0.0, old) - dot(old[:, rows], new)
            work[m, rows] = new


def solve_kernel(pred, moved, out, work):
    lo, hi = slice(0, HALF), slice(HALF, 2 * HALF)
    for m in range(2):
        work[m] = pred[m, lo, lo]
    half_inverse(work)
    wide, rest = [], []
    for m in range(2):
        rhs = jnp.concatenate([pred[m, lo, hi], moved[m, lo]], axis=1)
        w = dot(work[m], rhs)
        s = jnp.concatenate([pred[m, hi, hi], moved[m, hi]], axis=1) - dot(pred[m, hi, lo], w)
        wide.append(w)
        rest.append(s[:, HALF:])
        work[m] = s[:, :HALF]
    half_inverse(work)
    for m in range(2):
        h2 = dot(work[m], rest[m])
        out[m, hi] = h2
        out[m, lo] = wide[m][:, HALF:] - dot(wide[m][:, :HALF], h2)


def solve(pred, moved):
    return pl.pallas_call(
        solve_kernel,
        out_shape=jax.ShapeDtypeStruct(moved.shape, jnp.float32),
        in_specs=[pl.BlockSpec(memory_space=pltpu.VMEM)] * 2,
        out_specs=pl.BlockSpec(memory_space=pltpu.VMEM),
        scratch_shapes=[pltpu.VMEM((2, HALF, HALF), jnp.float32)],
        compiler_params=pltpu.CompilerParams(vmem_limit_bytes=32 * 1024 * 1024),
    )(pred, moved)


NS = 256
TOP = 192
LOW = NS - TOP
OFFSET = LOW + HALF
DIAG = OFFSET + 1
PART = OFFSET + EXTRA


def flipped(matrix):
    return jnp.swapaxes(matrix, -1, -2)


def tdot(left, right):
    return lax.dot_general(
        left, right, (((0,), (0,)), ((), ())),
        precision=lax.Precision.HIGHEST, preferred_element_type=jnp.float32,
    )


def row_col():
    return (
        lax.broadcasted_iota(jnp.int32, (HALF, HALF), 0),
        lax.broadcasted_iota(jnp.int32, (HALF, HALF), 1),
    )


def packed(upper, corner):
    r, c = row_col()
    both = jnp.where(r >= c, upper[:, :HALF], corner)
    diag = jnp.sum(jnp.where(r == c, corner, 0.0), axis=0, keepdims=True)
    return jnp.concatenate([upper[:, HALF:], both], axis=1), diag


def unpacked(half, diag):
    r, c = row_col()
    right, both = half[:, :HALF], half[:, HALF:]
    turned = both.T
    left = jnp.where(r >= c, both, turned)
    corner = jnp.where(r < c, both, jnp.where(r == c, diag, turned))
    return jnp.concatenate(
        [jnp.concatenate([left, right], axis=1), jnp.concatenate([right.T, corner], axis=1)], axis=0
    )


def sandwich(inner, gain):
    first = dot(inner, gain)
    upper = tdot(gain[:, :HALF], first)
    corner = tdot(gain[:, HALF:], first[:, HALF:])
    return packed(upper, corner)


def diag_row(diag):
    return jnp.concatenate([diag, jnp.zeros((1, NS - HALF), jnp.float32)], axis=1)


def store_held(out, base, half, diag, offset):
    out[base : base + HALF] = half
    tail = jnp.concatenate(
        [offset, diag_row(diag), jnp.zeros((EXTRA - 2, NS), jnp.float32)], axis=0
    )
    out[base + HALF : base + HALF + EXTRA] = tail


def chip_kernel(core, turned, held, other_turned, other_held, out):
    @pl.when(core[0] == 0)
    def _():
        out[:TOP] = dot(other_turned[:TOP], turned[...])
        out[TOP:] = jnp.zeros((PART - TOP, NS), jnp.float32)

    @pl.when(core[0] == 1)
    def _():
        gain = other_turned[...]
        out[:LOW] = dot(turned[TOP:], gain)
        half, diag = sandwich(held[:NS], gain)
        own, own_diag = packed(other_held[:HALF], other_held[HALF:NS, HALF:])
        tail = dot(held[NS:], gain) + other_held[NS:]
        store_held(out, LOW, half + own, diag + own_diag, tail[:1])


def join_kernel(core, got, mine, passed, out):
    @pl.when(core[0] == 0)
    def _():
        gain = jnp.concatenate([mine[:TOP], passed[:LOW]], axis=0)
        out[:TOP] = dot(got[:TOP], gain)
        out[TOP:] = jnp.zeros((PART - TOP, NS), jnp.float32)

    @pl.when(core[0] == 1)
    def _():
        gain = jnp.concatenate([passed[:TOP], mine[:LOW]], axis=0)
        out[:LOW] = dot(got[:LOW], gain)
        inner = unpacked(got[LOW:OFFSET], got[DIAG : DIAG + 1, :HALF])
        half, diag = sandwich(inner, gain)
        tail = dot(got[OFFSET:], gain)
        store_held(
            out, LOW, half + mine[LOW:OFFSET], diag + mine[DIAG : DIAG + 1, :HALF],
            tail[:1] + mine[OFFSET : OFFSET + 1],
        )


def last_kernel(core, got, mine, passed, out):
    @pl.when(core[0] == 0)
    def _():
        out[...] = jnp.zeros(out.shape, jnp.float32)

    @pl.when(core[0] == 1)
    def _():
        gain = jnp.concatenate([passed[:TOP], mine[:LOW]], axis=0)
        inner = unpacked(got[:HALF], got[HALF + 1 : HALF + 2, :HALF])
        half, diag = sandwich(inner, gain)
        tail = dot(got[HALF:], gain)
        store_held(
            out, 0, half + mine[LOW:OFFSET], diag + mine[DIAG : DIAG + 1, :HALF],
            tail[:1] + mine[OFFSET : OFFSET + 1],
        )


def end_kernel(after, turned0, held0, turned1, held1, cov, mean):
    inner = unpacked(after[:HALF], after[HALF + 1 : HALF + 2, :HALF])
    for i, (turned, held) in enumerate(((turned0, held0), (turned1, held1))):
        gain = turned[...]
        cov[i] = tdot(gain, dot(inner, gain)) + held[:NS]
        mean[i : i + 1] = (dot(after[HALF:], gain) + held[NS:])[:1]


def call(kernel, shapes, scalar, *arrays):
    vmem = pl.BlockSpec(memory_space=pltpu.VMEM)
    smem = pl.BlockSpec(memory_space=pltpu.SMEM)
    scalars = [] if scalar is None else [scalar]
    outs = [jax.ShapeDtypeStruct(s, jnp.float32) for s in shapes]
    done = pl.pallas_call(
        kernel,
        out_shape=outs,
        in_specs=[smem] * len(scalars) + [vmem] * len(arrays),
        out_specs=[vmem] * len(outs),
        compiler_params=pltpu.CompilerParams(vmem_limit_bytes=32 * 1024 * 1024),
    )(*scalars, *arrays)
    return done if len(outs) > 1 else done[0]


def product(left, right):
    return jnp.matmul(left, right, precision=lax.Precision.HIGHEST)


def grown(matrix, row):
    return jnp.concatenate([matrix, jnp.broadcast_to(row, (EXTRA, row.shape[-1]))], axis=0)


def applied(turned, held_next, held):
    width = turned.shape[0]
    first = product(held_next, turned)
    square = product(flipped(turned), first[:width]) + held[:width]
    return jnp.concatenate([square, first[width:] + held[width:]], axis=0)


def local(filt_mean, filt_cov, noise_cov, transition):
    devices = lax.axis_size(AXES)
    chips = devices // 2
    place = lax.axis_index(AXES)
    core = place % 2
    is_first = core == 0
    which = core.astype(jnp.int32)[None]
    moved = product(transition, filt_cov)
    predicted = product(moved, transition.T) + noise_cov
    solved = solve(predicted, moved)
    final = (place == devices - 1) & (jnp.arange(2) == 1)
    solved = jnp.where(final[:, None, None], 0.0, solved)
    ahead = product(filt_mean, transition.T)
    offset = filt_mean - product(ahead[:, None, :], solved)[:, 0]
    remainder = filt_cov - product(flipped(solved), moved)
    turned = [solved[0], solved[1]]
    held = [grown(remainder[0], offset[0]), grown(remainder[1], offset[1])]
    both_turned = product(turned[1], turned[0])
    both_held = applied(turned[0], held[1], held[0])

    swap = [(p, p ^ 1) for p in range(devices)]

    def swapped(rows):
        return lax.ppermute(rows, AXES, swap)

    other_turned = swapped(both_turned)
    other_held = swapped(both_held)
    chip = call(chip_kernel, [(PART, NS)], which, both_turned, both_held, other_turned, other_held)
    late = [jnp.where(is_first, product(other_turned, t), t) for t in (both_turned, turned[1])]
    late_held = [
        jnp.where(is_first, applied(t, other_held, h), h)
        for t, h in ((both_turned, both_held), (turned[1], held[1]))
    ]

    def fetched(rows, stride, cores):
        return lax.ppermute(
            rows, AXES, [(2 * (c + stride) + k, 2 * c + k) for c in range(chips - stride) for k in cores]
        )

    mine = fetched(chip, 1, (0, 1))
    got = fetched(chip, 2, (0, 1))
    stride = 2
    passed = swapped(mine[:TOP])
    mine = call(join_kernel, [(PART, NS)], which, got, mine, passed)
    while 2 * stride < chips:
        got = fetched(mine, stride, (0, 1))
        passed = swapped(mine[:TOP])
        mine = call(join_kernel, [(PART, NS)], which, got, mine, passed)
        stride *= 2
    got = fetched(mine[LOW:], stride, (1,))
    passed = swapped(mine[:TOP])
    after = call(last_kernel, [(HALF + EXTRA, NS)], which, got, mine, passed)
    to_first = lax.ppermute(after, AXES, [(2 * c + 1, 2 * c) for c in range(chips)])
    after = jnp.where(is_first, to_first, after)
    smooth_cov, smooth_mean = call(
        end_kernel, [(2, NS, NS), (2, NS)], None, after, late[0], late_held[0], late[1], late_held[1]
    )
    return (smooth_mean, smooth_cov)


def solution(mesh):
    in_specs = (P(AXES, None), P(AXES, None, None), P(AXES, None, None), P())
    out_specs = (P(AXES, None), P(AXES, None, None))
    return jax.shard_map(local, mesh=mesh, in_specs=in_specs, out_specs=out_specs, check_vma=False)
```

```python
import jax
import jax.numpy as jnp
from jax import lax
from jax.experimental import pallas as pl
from jax.experimental.pallas import tpu as pltpu
from jax.sharding import PartitionSpec as P

AXES = ("grp", "dev")
EXTRA = 8

BASE = 32
HALF = 128


def dot(left, right):
    return jnp.dot(left, right, precision=lax.Precision.HIGHEST, preferred_element_type=jnp.float32)


def base_inverse(first, second):
    unit = (lax.broadcasted_iota(jnp.int32, (BASE, BASE), 0) == lax.broadcasted_iota(jnp.int32, (BASE, BASE), 1)).astype(jnp.float32)
    whole = jnp.concatenate([first, unit, second, unit], axis=1)
    tiles = [whole[8 * i : 8 * i + 8] for i in range(BASE // 8)]
    lane = lax.broadcasted_iota(jnp.int32, (8, 128), 1)
    sub = lax.broadcasted_iota(jnp.int32, (8, 128), 0)
    for q in range(BASE // 8):
        cols = []
        for j in range(8):
            at = 8 * q + j
            cols.append([
                jnp.where(lane < 64, jnp.broadcast_to(t[:, at : at + 1], (8, 128)), jnp.broadcast_to(t[:, 64 + at : 65 + at], (8, 128)))
                for t in tiles
            ])
        for k in range(8):
            def row(t):
                return jnp.broadcast_to(t[k : k + 1], (8, 128))
            ratio = 1.0 / row(cols[k][q])
            scaled = row(tiles[q]) * ratio
            factors = [row(cols[j][q]) * ratio for j in range(k + 1, 8)]
            down = list(cols[k])
            down[q] = down[q] - jnp.where(sub == k, 1.0, 0.0)
            tiles = [t - d * scaled for t, d in zip(tiles, down)]
            for j, f in zip(range(k + 1, 8), factors):
                cols[j] = [c - d * f for c, d in zip(cols[j], down)]
    whole = jnp.concatenate(tiles, axis=0)
    return whole[:, BASE : 2 * BASE], whole[:, 64 + BASE : 64 + 2 * BASE]


def half_inverse(work):
    for j in range(HALF // BASE):
        rows = slice(BASE * j, BASE * j + BASE)
        inv = base_inverse(work[0, rows, rows], work[1, rows, rows])
        lane = lax.broadcasted_iota(jnp.int32, (HALF, HALF), 1)
        inside = (lane >= BASE * j) & (lane < BASE * (j + 1))
        r = lax.broadcasted_iota(jnp.int32, (BASE, HALF), 0)
        c = lax.broadcasted_iota(jnp.int32, (BASE, HALF), 1)
        for m in range(2):
            old = work[m]
            top = jnp.where(inside[:BASE], (c == r + BASE * j).astype(jnp.float32), old[rows])
            new = dot(inv[m], top)
            work[m] = jnp.where(inside, 0.0, old) - dot(old[:, rows], new)
            work[m, rows] = new


def solve_kernel(pred, moved, out, work):
    lo, hi = slice(0, HALF), slice(HALF, 2 * HALF)
    for m in range(2):
        work[m] = pred[m, lo, lo]
    half_inverse(work)
    wide, rest = [], []
    for m in range(2):
        rhs = jnp.concatenate([pred[m, lo, hi], moved[m, lo]], axis=1)
        w = dot(work[m], rhs)
        s = jnp.concatenate([pred[m, hi, hi], moved[m, hi]], axis=1) - dot(pred[m, hi, lo], w)
        wide.append(w)
        rest.append(s[:, HALF:])
        work[m] = s[:, :HALF]
    half_inverse(work)
    for m in range(2):
        h2 = dot(work[m], rest[m])
        out[m, hi] = h2
        out[m, lo] = wide[m][:, HALF:] - dot(wide[m][:, :HALF], h2)


def solve(pred, moved):
    return pl.pallas_call(
        solve_kernel,
        out_shape=jax.ShapeDtypeStruct(moved.shape, jnp.float32),
        in_specs=[pl.BlockSpec(memory_space=pltpu.VMEM)] * 2,
        out_specs=pl.BlockSpec(memory_space=pltpu.VMEM),
        scratch_shapes=[pltpu.VMEM((2, HALF, HALF), jnp.float32)],
        compiler_params=pltpu.CompilerParams(vmem_limit_bytes=32 * 1024 * 1024),
    )(pred, moved)


NS = 256
TOP = 192
LOW = NS - TOP
OFFSET = LOW + HALF
DIAG = OFFSET + 1
PART = OFFSET + EXTRA


def flipped(matrix):
    return jnp.swapaxes(matrix, -1, -2)


def halves(value):
    high = value.astype(jnp.bfloat16)
    return high, (value - high.astype(jnp.float32)).astype(jnp.bfloat16)


def three(left, right, dims):
    lh, ll = halves(left)
    rh, rl = halves(right)

    def one(a, b):
        return lax.dot_general(a, b, (dims, ((), ())), preferred_element_type=jnp.float32)

    return one(lh, rh) + (one(lh, rl) + one(ll, rh))


def mdot(left, right):
    return three(left, right, ((1,), (0,)))


def tdot(left, right):
    return three(left, right, ((0,), (0,)))


def row_col():
    return (
        lax.broadcasted_iota(jnp.int32, (HALF, HALF), 0),
        lax.broadcasted_iota(jnp.int32, (HALF, HALF), 1),
    )


def packed(upper, corner):
    r, c = row_col()
    both = jnp.where(r >= c, upper[:, :HALF], corner)
    diag = jnp.sum(jnp.where(r == c, corner, 0.0), axis=0, keepdims=True)
    return jnp.concatenate([upper[:, HALF:], both], axis=1), diag


def unpacked(half, diag):
    r, c = row_col()
    right, both = half[:, :HALF], half[:, HALF:]
    turned = both.T
    left = jnp.where(r >= c, both, turned)
    corner = jnp.where(r < c, both, jnp.where(r == c, diag, turned))
    return jnp.concatenate(
        [jnp.concatenate([left, right], axis=1), jnp.concatenate([right.T, corner], axis=1)], axis=0
    )


def sandwich(inner, gain):
    first = mdot(inner, gain)
    upper = tdot(gain[:, :HALF], first)
    corner = tdot(gain[:, HALF:], first[:, HALF:])
    return packed(upper, corner)


def diag_row(diag):
    return jnp.concatenate([diag, jnp.zeros((1, NS - HALF), jnp.float32)], axis=1)


def store_held(out, base, half, diag, offset):
    out[base : base + HALF] = half
    tail = jnp.concatenate(
        [offset, diag_row(diag), jnp.zeros((EXTRA - 2, NS), jnp.float32)], axis=0
    )
    out[base + HALF : base + HALF + EXTRA] = tail


def chip_kernel(core, turned, held, other_turned, other_held, out):
    @pl.when(core[0] == 0)
    def _():
        out[:TOP] = mdot(other_turned[:TOP], turned[...])
        out[TOP:] = jnp.zeros((PART - TOP, NS), jnp.float32)

    @pl.when(core[0] == 1)
    def _():
        gain = other_turned[...]
        out[:LOW] = mdot(turned[TOP:], gain)
        half, diag = sandwich(held[:NS], gain)
        own, own_diag = packed(other_held[:HALF], other_held[HALF:NS, HALF:])
        tail = mdot(held[NS:], gain) + other_held[NS:]
        store_held(out, LOW, half + own, diag + own_diag, tail[:1])


def join_kernel(core, got, mine, passed, out):
    @pl.when(core[0] == 0)
    def _():
        gain = jnp.concatenate([mine[:TOP], passed[:LOW]], axis=0)
        out[:TOP] = mdot(got[:TOP], gain)
        out[TOP:] = jnp.zeros((PART - TOP, NS), jnp.float32)

    @pl.when(core[0] == 1)
    def _():
        gain = jnp.concatenate([passed[:TOP], mine[:LOW]], axis=0)
        out[:LOW] = mdot(got[:LOW], gain)
        inner = unpacked(got[LOW:OFFSET], got[DIAG : DIAG + 1, :HALF])
        half, diag = sandwich(inner, gain)
        tail = mdot(got[OFFSET:], gain)
        store_held(
            out, LOW, half + mine[LOW:OFFSET], diag + mine[DIAG : DIAG + 1, :HALF],
            tail[:1] + mine[OFFSET : OFFSET + 1],
        )


def late_kernel(core, mine, passed, turned0, held0, turned1, held1, gain0, rest0, gain1, rest1):
    first = core[0] == 0
    gain = jnp.where(
        first,
        jnp.concatenate([mine[:TOP], passed[:LOW]], axis=0),
        jnp.concatenate([passed[:TOP], mine[:LOW]], axis=0),
    )
    own = jnp.where(first, passed[LOW:], mine[LOW:])
    inner = unpacked(own[:HALF], own[HALF + 1 : HALF + 2, :HALF])
    for turned, held, full, rest in (
        (turned0[...], held0, gain0, rest0), (turned1[...], held1, gain1, rest1)
    ):
        full[...] = mdot(gain, turned)
        rest[:NS] = tdot(turned, mdot(inner, turned)) + held[:NS]
        rest[NS:] = mdot(own[HALF:], turned) + held[NS:]


def end_kernel(to_second, to_first, turned0, held0, turned1, held1, cov, mean):
    after = to_second[...] + to_first[...]
    inner = unpacked(after[:HALF], after[HALF + 1 : HALF + 2, :HALF])
    for i, (turned, held) in enumerate(((turned0, held0), (turned1, held1))):
        gain = turned[...]
        cov[i] = tdot(gain, mdot(inner, gain)) + held[:NS]
        mean[i : i + 1] = (mdot(after[HALF:], gain) + held[NS:])[:1]


def call(kernel, shapes, scalar, *arrays):
    vmem = pl.BlockSpec(memory_space=pltpu.VMEM)
    smem = pl.BlockSpec(memory_space=pltpu.SMEM)
    scalars = [] if scalar is None else [scalar]
    outs = [jax.ShapeDtypeStruct(s, jnp.float32) for s in shapes]
    done = pl.pallas_call(
        kernel,
        out_shape=outs,
        in_specs=[smem] * len(scalars) + [vmem] * len(arrays),
        out_specs=[vmem] * len(outs),
        compiler_params=pltpu.CompilerParams(vmem_limit_bytes=32 * 1024 * 1024),
    )(*scalars, *arrays)
    return done if len(outs) > 1 else done[0]


def product(left, right):
    return jnp.matmul(left, right, precision=lax.Precision.HIGHEST)


def grown(matrix, row):
    return jnp.concatenate([matrix, jnp.broadcast_to(row, (EXTRA, row.shape[-1]))], axis=0)


def applied(turned, held_next, held):
    width = turned.shape[0]
    first = product(held_next, turned)
    square = product(flipped(turned), first[:width]) + held[:width]
    return jnp.concatenate([square, first[width:] + held[width:]], axis=0)


def local(filt_mean, filt_cov, noise_cov, transition):
    devices = lax.axis_size(AXES)
    chips = devices // 2
    place = lax.axis_index(AXES)
    core = place % 2
    is_first = core == 0
    which = core.astype(jnp.int32)[None]
    moved = product(transition, filt_cov)
    predicted = product(moved, transition.T) + noise_cov
    solved = solve(predicted, moved)
    final = (place == devices - 1) & (jnp.arange(2) == 1)
    solved = jnp.where(final[:, None, None], 0.0, solved)
    ahead = product(filt_mean, transition.T)
    offset = filt_mean - product(ahead[:, None, :], solved)[:, 0]
    remainder = filt_cov - product(flipped(solved), moved)
    turned = [solved[0], solved[1]]
    held = [grown(remainder[0], offset[0]), grown(remainder[1], offset[1])]
    both_turned = product(turned[1], turned[0])
    both_held = applied(turned[0], held[1], held[0])

    swap = [(p, p ^ 1) for p in range(devices)]

    def swapped(rows):
        return lax.ppermute(rows, AXES, swap)

    other_turned = swapped(both_turned)
    other_held = swapped(both_held)
    chip = call(chip_kernel, [(PART, NS)], which, both_turned, both_held, other_turned, other_held)
    late = [jnp.where(is_first, product(other_turned, t), t) for t in (both_turned, turned[1])]
    late_held = [
        jnp.where(is_first, applied(t, other_held, h), h)
        for t, h in ((both_turned, both_held), (turned[1], held[1]))
    ]

    def fetched(rows, stride, cores):
        return lax.ppermute(
            rows, AXES, [(2 * (c + stride) + k, 2 * c + k) for c in range(chips - stride) for k in cores]
        )

    mine = fetched(chip, 1, (0, 1))
    got = fetched(chip, 2, (0, 1))
    stride = 2
    passed = swapped(mine[:TOP])
    mine = call(join_kernel, [(PART, NS)], which, got, mine, passed)
    while 2 * stride < chips:
        got = fetched(mine, stride, (0, 1))
        passed = swapped(mine[:TOP])
        mine = call(join_kernel, [(PART, NS)], which, got, mine, passed)
        stride *= 2
    tails = mine[LOW:]
    to_second, to_first = [
        lax.ppermute(tails, AXES, [(2 * (c + stride) + 1, 2 * c + k) for c in range(chips - stride)])
        for k in (1, 0)
    ]
    passed = swapped(mine)
    square, wide = (NS, NS), (NS + EXTRA, NS)
    gain0, rest0, gain1, rest1 = call(
        late_kernel, [square, wide, square, wide], which, mine, passed,
        late[0], late_held[0], late[1], late_held[1],
    )
    smooth_cov, smooth_mean = call(
        end_kernel, [(2, NS, NS), (2, NS)], None, to_second, to_first, gain0, rest0, gain1, rest1
    )
    return (smooth_mean, smooth_cov)


def solution(mesh):
    in_specs = (P(AXES, None), P(AXES, None, None), P(AXES, None, None), P())
    out_specs = (P(AXES, None), P(AXES, None, None))
    return jax.shard_map(local, mesh=mesh, in_specs=in_specs, out_specs=out_specs, check_vma=False)
```

```python
import jax
import jax.numpy as jnp
from jax import lax
from jax.experimental import pallas as pl
from jax.experimental.pallas import tpu as pltpu
from jax.sharding import PartitionSpec as P

AXES = ("grp", "dev")
EXTRA = 8

BASE = 16
HALF = 128


def dot(left, right):
    return jnp.dot(left, right, precision=lax.Precision.HIGHEST, preferred_element_type=jnp.float32)


def eliminated(tops, base):
    tiles = [[t[8 * i : 8 * i + 8] for i in range(BASE // 8)] for t in tops]
    lane = lax.broadcasted_iota(jnp.int32, (8, HALF), 1)
    sub = lax.broadcasted_iota(jnp.int32, (8, HALF), 0)

    def spread(row):
        return jnp.broadcast_to(row, (8, HALF))

    for q in range(BASE // 8):
        cols = []
        for m in range(2):
            at = base + 8 * q
            cols.append([[spread(t[:, at + j : at + j + 1]) for t in tiles[m]] for j in range(8)])
        for k in range(8):
            here = lane == base + 8 * q + k
            unit = jnp.where(sub == k, 1.0, 0.0)
            for m in range(2):
                col, tile = cols[m], tiles[m]
                ratio = 1.0 / (spread(col[k][q][k : k + 1]))
                scaled = jnp.where(here, ratio, spread(tile[q][k : k + 1]) * ratio)
                factors = [spread(col[j][q][k : k + 1]) * ratio for j in range(k + 1, 8)]
                down = list(col[k])
                down[q] = down[q] - unit
                for i in range(BASE // 8):
                    old = jnp.where(here, unit if i == q else 0.0, tile[i])
                    tile[i] = old - down[i] * scaled
                for j, f in zip(range(k + 1, 8), factors):
                    col[j] = [c - d * f for c, d in zip(col[j], down)]
    return [jnp.concatenate(t, axis=0) for t in tiles]


def less_product(rows, base, inside, new):
    parts = []
    for i in range(BASE // 8):
        old = rows[8 * i : 8 * i + 8]
        terms = [
            jnp.broadcast_to(old[:, base + k : base + k + 1], (8, HALF)) * jnp.broadcast_to(new[k : k + 1], (8, HALF))
            for k in range(BASE)
        ]
        while len(terms) > 1:
            terms = [a + b for a, b in zip(terms[::2], terms[1::2])]
        parts.append(jnp.where(inside[:8], 0.0, old) - terms[0])
    return jnp.concatenate(parts, axis=0)


def half_inverse(pair):
    lane = lax.broadcasted_iota(jnp.int32, (BASE, HALF), 1)
    count = HALF // BASE
    pair = [[p[BASE * i : BASE * i + BASE] for i in range(count)] for p in pair]
    for j in range(count):
        rows = slice(BASE * j, BASE * j + BASE)
        inside = (lane >= BASE * j) & (lane < BASE * (j + 1))
        news = eliminated([p[j] for p in pair], BASE * j)
        for m in range(2):
            first = (j + 1) % count
            rest = [i for i in range(count) if i not in (j, first)]
            old = pair[m]
            new = [None] * count
            new[j] = news[m]
            new[first] = less_product(old[first], BASE * j, inside, news[m])
            tall = jnp.concatenate([old[i][:, rows] for i in rest], axis=0)
            tall = dot(tall, news[m])
            for n, i in enumerate(rest):
                new[i] = jnp.where(inside, 0.0, old[i]) - tall[BASE * n : BASE * n + BASE]
            pair[m] = new
    return [jnp.concatenate(p, axis=0) for p in pair]


def solved_pair(pred, moved):
    lo, hi = slice(0, HALF), slice(HALF, 2 * HALF)
    inv = half_inverse([p[lo, lo] for p in pred])
    wide, corner, out = [], [], []
    for m in range(2):
        wide.append(dot(inv[m], jnp.concatenate([pred[m][lo, hi], moved[m][lo]], axis=1)))
        corner.append(pred[m][hi, hi] - dot(pred[m][hi, lo], wide[m][:, :HALF]))
    inv = half_inverse(corner)
    for m in range(2):
        rest = moved[m][hi] - dot(pred[m][hi, lo], wide[m][:, HALF:])
        low = dot(inv[m], rest)
        top = wide[m][:, HALF:] - dot(wide[m][:, :HALF], low)
        out.append(jnp.concatenate([top, low], axis=0))
    return out


NS = 256
TOP = 192
LOW = NS - TOP
OFFSET = LOW + HALF
DIAG = OFFSET + 1
PART = OFFSET + EXTRA


def flipped(matrix):
    return jnp.swapaxes(matrix, -1, -2)


def halves(value):
    high = value.astype(jnp.bfloat16)
    return high, (value - high.astype(jnp.float32)).astype(jnp.bfloat16)


def three(left, right, dims):
    lh, ll = halves(left)
    rh, rl = halves(right)

    def one(a, b):
        return lax.dot_general(a, b, (dims, ((), ())), preferred_element_type=jnp.float32)

    return one(lh, rh) + (one(lh, rl) + one(ll, rh))


def mdot(left, right):
    return three(left, right, ((1,), (0,)))


def tdot(left, right):
    return three(left, right, ((0,), (0,)))


def row_col():
    return (
        lax.broadcasted_iota(jnp.int32, (HALF, HALF), 0),
        lax.broadcasted_iota(jnp.int32, (HALF, HALF), 1),
    )


def packed(upper, corner):
    r, c = row_col()
    both = jnp.where(r >= c, upper[:, :HALF], corner)
    diag = jnp.sum(jnp.where(r == c, corner, 0.0), axis=0, keepdims=True)
    return jnp.concatenate([upper[:, HALF:], both], axis=1), diag


def unpacked(half, diag):
    r, c = row_col()
    right, both = half[:, :HALF], half[:, HALF:]
    turned = both.T
    left = jnp.where(r >= c, both, turned)
    corner = jnp.where(r < c, both, jnp.where(r == c, diag, turned))
    return jnp.concatenate(
        [jnp.concatenate([left, right], axis=1), jnp.concatenate([right.T, corner], axis=1)], axis=0
    )


def sandwich(inner, gain):
    first = mdot(inner, gain)
    upper = tdot(gain[:, :HALF], first)
    corner = tdot(gain[:, HALF:], first[:, HALF:])
    return packed(upper, corner)


def diag_row(diag):
    return jnp.concatenate([diag, jnp.zeros((1, NS - HALF), jnp.float32)], axis=1)


def store_held(out, base, half, diag, offset):
    out[base : base + HALF] = half
    tail = jnp.concatenate(
        [offset, diag_row(diag), jnp.zeros((EXTRA - 2, NS), jnp.float32)], axis=0
    )
    out[base + HALF : base + HALF + EXTRA] = tail


def exact(left, right, dims):
    return lax.dot_general(
        left, right, (dims, ((), ())),
        precision=lax.Precision.HIGHEST, preferred_element_type=jnp.float32,
    )


def local_kernel(final, mean, cov, noise, transition, both, turned1, held1):
    step = transition[...]
    moved = [dot(step, cov[m]) for m in range(2)]
    pred = [exact(moved[m], step, ((1,), (1,))) + noise[m] for m in range(2)]
    gains = solved_pair(pred, moved)
    gains[1] = jnp.where(final[0] == 1, 0.0, gains[1])
    means = jnp.concatenate([mean[...], jnp.zeros((EXTRA - 2, NS), jnp.float32)], axis=0)
    ahead = exact(means, step, ((1,), (1,)))
    rests = [cov[m] - exact(gains[m], moved[m], ((0,), (0,))) for m in range(2)]
    offsets = [means - dot(ahead, gains[m]) for m in range(2)]
    turned1[...] = gains[1]
    held1[:NS] = rests[1]
    held1[NS:] = jnp.broadcast_to(offsets[1][1:2], (EXTRA, NS))
    both[:NS] = mdot(gains[1], gains[0])
    both[NS : 2 * NS] = tdot(gains[0], mdot(rests[1], gains[0])) + rests[0]
    second = mdot(offsets[1], gains[0])[1:2]
    both[2 * NS :] = jnp.broadcast_to(second + offsets[0][:1], (EXTRA, NS))


def chip_kernel(core, own, other, out):
    @pl.when(core[0] == 0)
    def _():
        out[:TOP] = mdot(other[:TOP], own[:NS])
        out[TOP:] = jnp.zeros((PART - TOP, NS), jnp.float32)

    @pl.when(core[0] == 1)
    def _():
        gain = other[:NS]
        out[:LOW] = mdot(own[TOP:NS], gain)
        half, diag = sandwich(own[NS : 2 * NS], gain)
        add, add_diag = packed(other[NS : NS + HALF], other[NS + HALF : 2 * NS, HALF:])
        tail = mdot(own[2 * NS :], gain) + other[2 * NS :]
        store_held(out, LOW, half + add, diag + add_diag, tail[:1])


def join_kernel(core, got, mine, passed, out):
    @pl.when(core[0] == 0)
    def _():
        gain = jnp.concatenate([mine[:TOP], passed[:LOW]], axis=0)
        out[:TOP] = mdot(got[:TOP], gain)
        out[TOP:] = jnp.zeros((PART - TOP, NS), jnp.float32)

    @pl.when(core[0] == 1)
    def _():
        gain = jnp.concatenate([passed[:TOP], mine[:LOW]], axis=0)
        out[:LOW] = mdot(got[:LOW], gain)
        inner = unpacked(got[LOW:OFFSET], got[DIAG : DIAG + 1, :HALF])
        half, diag = sandwich(inner, gain)
        tail = mdot(got[OFFSET:], gain)
        store_held(
            out, LOW, half + mine[LOW:OFFSET], diag + mine[DIAG : DIAG + 1, :HALF],
            tail[:1] + mine[OFFSET : OFFSET + 1],
        )


def late_kernel(core, mine, passed, turned0, held0, turned1, held1, gain0, rest0, gain1, rest1):
    first = core[0] == 0
    gain = jnp.where(
        first,
        jnp.concatenate([mine[:TOP], passed[:LOW]], axis=0),
        jnp.concatenate([passed[:TOP], mine[:LOW]], axis=0),
    )
    own = jnp.where(first, passed[LOW:], mine[LOW:])
    inner = unpacked(own[:HALF], own[HALF + 1 : HALF + 2, :HALF])
    for turned, held, full, rest in (
        (turned0[...], held0, gain0, rest0), (turned1[...], held1, gain1, rest1)
    ):
        full[...] = mdot(gain, turned)
        rest[:NS] = tdot(turned, mdot(inner, turned)) + held[:NS]
        rest[NS:] = mdot(own[HALF:], turned) + held[NS:]


def end_kernel(to_second, to_first, turned0, held0, turned1, held1, cov, mean):
    after = to_second[...] + to_first[...]
    inner = unpacked(after[:HALF], after[HALF + 1 : HALF + 2, :HALF])
    for i, (turned, held) in enumerate(((turned0, held0), (turned1, held1))):
        gain = turned[...]
        cov[i] = tdot(gain, mdot(inner, gain)) + held[:NS]
        mean[i : i + 1] = (mdot(after[HALF:], gain) + held[NS:])[:1]


def call(kernel, shapes, scalar, *arrays):
    vmem = pl.BlockSpec(memory_space=pltpu.VMEM)
    smem = pl.BlockSpec(memory_space=pltpu.SMEM)
    scalars = [] if scalar is None else [scalar]
    outs = [jax.ShapeDtypeStruct(s, jnp.float32) for s in shapes]
    done = pl.pallas_call(
        kernel,
        out_shape=outs,
        in_specs=[smem] * len(scalars) + [vmem] * len(arrays),
        out_specs=[vmem] * len(outs),
        compiler_params=pltpu.CompilerParams(vmem_limit_bytes=32 * 1024 * 1024),
    )(*scalars, *arrays)
    return done if len(outs) > 1 else done[0]


def product(left, right):
    return jnp.matmul(left, right, precision=lax.Precision.HIGHEST)


def applied(turned, held_next, held):
    width = turned.shape[0]
    first = product(held_next, turned)
    square = product(flipped(turned), first[:width]) + held[:width]
    return jnp.concatenate([square, first[width:] + held[width:]], axis=0)


def local(filt_mean, filt_cov, noise_cov, transition):
    devices = lax.axis_size(AXES)
    chips = devices // 2
    place = lax.axis_index(AXES)
    core = place % 2
    is_first = core == 0
    which = core.astype(jnp.int32)[None]
    final = (place == devices - 1).astype(jnp.int32)[None]
    wide = (NS + EXTRA, NS)
    both, turned1, held1 = call(
        local_kernel, [(2 * NS + EXTRA, NS), (NS, NS), wide], final,
        filt_mean, filt_cov, noise_cov, transition,
    )

    swap = [(p, p ^ 1) for p in range(devices)]

    def swapped(rows):
        return lax.ppermute(rows, AXES, swap)

    other = swapped(both)
    chip = call(chip_kernel, [(PART, NS)], which, both, other)
    both_turned, both_held = both[:NS], both[NS:]
    late = [jnp.where(is_first, product(other[:NS], t), t) for t in (both_turned, turned1)]
    late_held = [
        jnp.where(is_first, applied(t, other[NS:], h), h)
        for t, h in ((both_turned, both_held), (turned1, held1))
    ]

    def fetched(rows, stride, cores):
        return lax.ppermute(
            rows, AXES, [(2 * (c + stride) + k, 2 * c + k) for c in range(chips - stride) for k in cores]
        )

    mine = fetched(chip, 1, (0, 1))
    got = fetched(chip, 2, (0, 1))
    stride = 2
    passed = swapped(mine[:TOP])
    mine = call(join_kernel, [(PART, NS)], which, got, mine, passed)
    while 2 * stride < chips:
        got = fetched(mine, stride, (0, 1))
        passed = swapped(mine[:TOP])
        mine = call(join_kernel, [(PART, NS)], which, got, mine, passed)
        stride *= 2
    tails = mine[LOW:]
    to_second, to_first = [
        lax.ppermute(tails, AXES, [(2 * (c + stride) + 1, 2 * c + k) for c in range(chips - stride)])
        for k in (1, 0)
    ]
    passed = swapped(mine)
    square = (NS, NS)
    gain0, rest0, gain1, rest1 = call(
        late_kernel, [square, wide, square, wide], which, mine, passed,
        late[0], late_held[0], late[1], late_held[1],
    )
    smooth_cov, smooth_mean = call(
        end_kernel, [(2, NS, NS), (2, NS)], None, to_second, to_first, gain0, rest0, gain1, rest1
    )
    return (smooth_mean, smooth_cov)


def solution(mesh):
    in_specs = (P(AXES, None), P(AXES, None, None), P(AXES, None, None), P())
    out_specs = (P(AXES, None), P(AXES, None, None))
    return jax.shard_map(local, mesh=mesh, in_specs=in_specs, out_specs=out_specs, check_vma=False)
```

```python
import jax
import jax.numpy as jnp
from jax import lax
from jax.experimental import pallas as pl
from jax.experimental.pallas import tpu as pltpu
from jax.sharding import PartitionSpec as P

AXES = ("grp", "dev")
EXTRA = 8

BASE = 16
HALF = 128


def dot(left, right):
    return jnp.dot(left, right, precision=lax.Precision.HIGHEST, preferred_element_type=jnp.float32)


def eliminated(tops, base):
    tiles = [[t[8 * i : 8 * i + 8] for i in range(BASE // 8)] for t in tops]
    lane = lax.broadcasted_iota(jnp.int32, (8, HALF), 1)
    sub = lax.broadcasted_iota(jnp.int32, (8, HALF), 0)

    def spread(row):
        return jnp.broadcast_to(row, (8, HALF))

    for q in range(BASE // 8):
        cols = []
        for m in range(2):
            at = base + 8 * q
            cols.append([[spread(t[:, at + j : at + j + 1]) for t in tiles[m]] for j in range(8)])
        for k in range(8):
            here = lane == base + 8 * q + k
            unit = jnp.where(sub == k, 1.0, 0.0)
            for m in range(2):
                col, tile = cols[m], tiles[m]
                ratio = 1.0 / (spread(col[k][q][k : k + 1]))
                scaled = jnp.where(here, ratio, spread(tile[q][k : k + 1]) * ratio)
                factors = [spread(col[j][q][k : k + 1]) * ratio for j in range(k + 1, 8)]
                down = list(col[k])
                down[q] = down[q] - unit
                for i in range(BASE // 8):
                    old = jnp.where(here, unit if i == q else 0.0, tile[i])
                    tile[i] = old - down[i] * scaled
                for j, f in zip(range(k + 1, 8), factors):
                    col[j] = [c - d * f for c, d in zip(col[j], down)]
    return [jnp.concatenate(t, axis=0) for t in tiles]


def less_product(rows, base, inside, new):
    parts = []
    for i in range(BASE // 8):
        old = rows[8 * i : 8 * i + 8]
        terms = [
            jnp.broadcast_to(old[:, base + k : base + k + 1], (8, HALF)) * jnp.broadcast_to(new[k : k + 1], (8, HALF))
            for k in range(BASE)
        ]
        while len(terms) > 1:
            terms = [a + b for a, b in zip(terms[::2], terms[1::2])]
        parts.append(jnp.where(inside[:8], 0.0, old) - terms[0])
    return jnp.concatenate(parts, axis=0)


def half_inverse(pair):
    lane = lax.broadcasted_iota(jnp.int32, (BASE, HALF), 1)
    count = HALF // BASE
    pair = [[p[BASE * i : BASE * i + BASE] for i in range(count)] for p in pair]
    for j in range(count):
        rows = slice(BASE * j, BASE * j + BASE)
        inside = (lane >= BASE * j) & (lane < BASE * (j + 1))
        news = eliminated([p[j] for p in pair], BASE * j)
        for m in range(2):
            first = (j + 1) % count
            rest = [i for i in range(count) if i not in (j, first)]
            old = pair[m]
            new = [None] * count
            new[j] = news[m]
            new[first] = less_product(old[first], BASE * j, inside, news[m])
            tall = jnp.concatenate([old[i][:, rows] for i in rest], axis=0)
            tall = dot(tall, news[m])
            for n, i in enumerate(rest):
                new[i] = jnp.where(inside, 0.0, old[i]) - tall[BASE * n : BASE * n + BASE]
            pair[m] = new
    return [jnp.concatenate(p, axis=0) for p in pair]


def solved_pair(pred, moved):
    lo, hi = slice(0, HALF), slice(HALF, 2 * HALF)
    inv = half_inverse([p[lo, lo] for p in pred])
    wide, corner, out = [], [], []
    for m in range(2):
        wide.append(dot(inv[m], jnp.concatenate([pred[m][lo, hi], moved[m][lo]], axis=1)))
        corner.append(pred[m][hi, hi] - dot(pred[m][hi, lo], wide[m][:, :HALF]))
    inv = half_inverse(corner)
    for m in range(2):
        rest = moved[m][hi] - dot(pred[m][hi, lo], wide[m][:, HALF:])
        low = dot(inv[m], rest)
        top = wide[m][:, HALF:] - dot(wide[m][:, :HALF], low)
        out.append(jnp.concatenate([top, low], axis=0))
    return out


NS = 256
TOP = 192
LOW = NS - TOP
OFFSET = LOW + HALF
DIAG = OFFSET + 1
PART = OFFSET + EXTRA


def flipped(matrix):
    return jnp.swapaxes(matrix, -1, -2)


def halves(value):
    high = value.astype(jnp.bfloat16)
    return high, (value - high.astype(jnp.float32)).astype(jnp.bfloat16)


def three(left, right, dims):
    lh, ll = halves(left)
    rh, rl = halves(right)

    def one(a, b):
        return lax.dot_general(a, b, (dims, ((), ())), preferred_element_type=jnp.float32)

    return one(lh, rh) + (one(lh, rl) + one(ll, rh))


def mdot(left, right):
    return three(left, right, ((1,), (0,)))


def tdot(left, right):
    return three(left, right, ((0,), (0,)))


def row_col():
    return (
        lax.broadcasted_iota(jnp.int32, (HALF, HALF), 0),
        lax.broadcasted_iota(jnp.int32, (HALF, HALF), 1),
    )


def packed(upper, corner):
    r, c = row_col()
    both = jnp.where(r >= c, upper[:, :HALF], corner)
    diag = jnp.sum(jnp.where(r == c, corner, 0.0), axis=0, keepdims=True)
    return jnp.concatenate([upper[:, HALF:], both], axis=1), diag


def unpacked(half, diag):
    r, c = row_col()
    right, both = half[:, :HALF], half[:, HALF:]
    turned = both.T
    left = jnp.where(r >= c, both, turned)
    corner = jnp.where(r < c, both, jnp.where(r == c, diag, turned))
    return jnp.concatenate(
        [jnp.concatenate([left, right], axis=1), jnp.concatenate([right.T, corner], axis=1)], axis=0
    )


def sandwich(inner, gain):
    first = mdot(inner, gain)
    upper = tdot(gain[:, :HALF], first)
    corner = tdot(gain[:, HALF:], first[:, HALF:])
    return packed(upper, corner)


def diag_row(diag):
    return jnp.concatenate([diag, jnp.zeros((1, NS - HALF), jnp.float32)], axis=1)


def store_held(out, base, half, diag, offset):
    out[base : base + HALF] = half
    tail = jnp.concatenate(
        [offset, diag_row(diag), jnp.zeros((EXTRA - 2, NS), jnp.float32)], axis=0
    )
    out[base + HALF : base + HALF + EXTRA] = tail


def exact(left, right, dims):
    return lax.dot_general(
        left, right, (dims, ((), ())),
        precision=lax.Precision.HIGHEST, preferred_element_type=jnp.float32,
    )


def local_kernel(
    final, mean_in, cov_in, noise_in, step_in, both, turned1, held1, mean, cov, noise, step_at, done
):
    moves = [(step_in, step_at), (cov_in.at[0], cov.at[0]), (cov_in.at[1], cov.at[1])]
    moves += [(noise_in.at[0], noise.at[0]), (noise_in.at[1], noise.at[1]), (mean_in, mean)]
    copies = [pltpu.make_async_copy(a, b, done.at[i]) for i, (a, b) in enumerate(moves)]
    for copy in copies:
        copy.start()
    copies[0].wait()
    step = step_at[...]
    moved = []
    for m in range(2):
        copies[1 + m].wait()
        moved.append(dot(step, cov[m]))
    for copy in copies[3:]:
        copy.wait()
    pred = [exact(moved[m], step, ((1,), (1,))) + noise[m] for m in range(2)]
    gains = solved_pair(pred, moved)
    gains[1] = jnp.where(final[0] == 1, 0.0, gains[1])
    means = jnp.concatenate([mean[...], jnp.zeros((EXTRA - 2, NS), jnp.float32)], axis=0)
    ahead = exact(means, step, ((1,), (1,)))
    rests = [cov[m] - exact(gains[m], moved[m], ((0,), (0,))) for m in range(2)]
    offsets = [means - dot(ahead, gains[m]) for m in range(2)]
    turned1[...] = gains[1]
    held1[:NS] = rests[1]
    held1[NS:] = jnp.broadcast_to(offsets[1][1:2], (EXTRA, NS))
    both[:NS] = mdot(gains[1], gains[0])
    both[NS : 2 * NS] = tdot(gains[0], mdot(rests[1], gains[0])) + rests[0]
    second = mdot(offsets[1], gains[0])[1:2]
    both[2 * NS :] = jnp.broadcast_to(second + offsets[0][:1], (EXTRA, NS))


def chip_kernel(core, own, other, out):
    @pl.when(core[0] == 0)
    def _():
        out[:TOP] = mdot(other[:TOP], own[:NS])
        out[TOP:] = jnp.zeros((PART - TOP, NS), jnp.float32)

    @pl.when(core[0] == 1)
    def _():
        gain = other[:NS]
        out[:LOW] = mdot(own[TOP:NS], gain)
        half, diag = sandwich(own[NS : 2 * NS], gain)
        add, add_diag = packed(other[NS : NS + HALF], other[NS + HALF : 2 * NS, HALF:])
        tail = mdot(own[2 * NS :], gain) + other[2 * NS :]
        store_held(out, LOW, half + add, diag + add_diag, tail[:1])


def join_kernel(core, got, mine, passed, out):
    @pl.when(core[0] == 0)
    def _():
        gain = jnp.concatenate([mine[:TOP], passed[:LOW]], axis=0)
        out[:TOP] = mdot(got[:TOP], gain)
        out[TOP:] = jnp.zeros((PART - TOP, NS), jnp.float32)

    @pl.when(core[0] == 1)
    def _():
        gain = jnp.concatenate([passed[:TOP], mine[:LOW]], axis=0)
        out[:LOW] = mdot(got[:LOW], gain)
        inner = unpacked(got[LOW:OFFSET], got[DIAG : DIAG + 1, :HALF])
        half, diag = sandwich(inner, gain)
        tail = mdot(got[OFFSET:], gain)
        store_held(
            out, LOW, half + mine[LOW:OFFSET], diag + mine[DIAG : DIAG + 1, :HALF],
            tail[:1] + mine[OFFSET : OFFSET + 1],
        )


def late_kernel(core, mine, passed, turned0, held0, turned1, held1, gain0, rest0, gain1, rest1):
    first = core[0] == 0
    gain = jnp.where(
        first,
        jnp.concatenate([mine[:TOP], passed[:LOW]], axis=0),
        jnp.concatenate([passed[:TOP], mine[:LOW]], axis=0),
    )
    own = jnp.where(first, passed[LOW:], mine[LOW:])
    inner = unpacked(own[:HALF], own[HALF + 1 : HALF + 2, :HALF])
    for turned, held, full, rest in (
        (turned0[...], held0, gain0, rest0), (turned1[...], held1, gain1, rest1)
    ):
        full[...] = mdot(gain, turned)
        rest[:NS] = tdot(turned, mdot(inner, turned)) + held[:NS]
        rest[NS:] = mdot(own[HALF:], turned) + held[NS:]


def end_kernel(to_second, to_first, turned0, held0, turned1, held1, cov_out, mean, cov, done):
    after = to_second[...] + to_first[...]
    inner = unpacked(after[:HALF], after[HALF + 1 : HALF + 2, :HALF])
    copies = [pltpu.make_async_copy(cov.at[i], cov_out.at[i], done.at[i]) for i in range(2)]
    for i, (turned, held) in enumerate(((turned0, held0), (turned1, held1))):
        gain = turned[...]
        cov[i] = tdot(gain, mdot(inner, gain)) + held[:NS]
        copies[i].start()
        mean[i : i + 1] = (mdot(after[HALF:], gain) + held[NS:])[:1]
    for copy in copies:
        copy.wait()


def call(kernel, shapes, scalar, *arrays, far_in=False, far_out=(), scratch=()):
    vmem = pl.BlockSpec(memory_space=pltpu.VMEM)
    far = pl.BlockSpec(memory_space=pltpu.HBM)
    smem = pl.BlockSpec(memory_space=pltpu.SMEM)
    scalars = [] if scalar is None else [scalar]
    outs = [jax.ShapeDtypeStruct(s, jnp.float32) for s in shapes]
    done = pl.pallas_call(
        kernel,
        out_shape=outs,
        in_specs=[smem] * len(scalars) + [far if far_in else vmem] * len(arrays),
        out_specs=[far if i in far_out else vmem for i in range(len(outs))],
        scratch_shapes=scratch,
        compiler_params=pltpu.CompilerParams(vmem_limit_bytes=32 * 1024 * 1024),
    )(*scalars, *arrays)
    return done if len(outs) > 1 else done[0]


def product(left, right):
    return jnp.matmul(left, right, precision=lax.Precision.HIGHEST)


def applied(turned, held_next, held):
    width = turned.shape[0]
    first = product(held_next, turned)
    square = product(flipped(turned), first[:width]) + held[:width]
    return jnp.concatenate([square, first[width:] + held[width:]], axis=0)


def local(filt_mean, filt_cov, noise_cov, transition):
    devices = lax.axis_size(AXES)
    chips = devices // 2
    place = lax.axis_index(AXES)
    core = place % 2
    is_first = core == 0
    which = core.astype(jnp.int32)[None]
    final = (place == devices - 1).astype(jnp.int32)[None]
    wide = (NS + EXTRA, NS)
    both, turned1, held1 = call(
        local_kernel, [(2 * NS + EXTRA, NS), (NS, NS), wide], final,
        *(pltpu.with_memory_space_constraint(a, pltpu.HBM) for a in (filt_mean, filt_cov, noise_cov, transition)),
        far_in=True,
        scratch=[
            *(pltpu.VMEM(a.shape, jnp.float32) for a in (filt_mean, filt_cov, noise_cov, transition)),
            pltpu.SemaphoreType.DMA((6,)),
        ],
    )

    swap = [(p, p ^ 1) for p in range(devices)]

    def swapped(rows):
        return lax.ppermute(rows, AXES, swap)

    other = swapped(both)
    chip = call(chip_kernel, [(PART, NS)], which, both, other)
    both_turned, both_held = both[:NS], both[NS:]
    late = [jnp.where(is_first, product(other[:NS], t), t) for t in (both_turned, turned1)]
    late_held = [
        jnp.where(is_first, applied(t, other[NS:], h), h)
        for t, h in ((both_turned, both_held), (turned1, held1))
    ]

    def fetched(rows, stride, cores):
        return lax.ppermute(
            rows, AXES, [(2 * (c + stride) + k, 2 * c + k) for c in range(chips - stride) for k in cores]
        )

    mine = fetched(chip, 1, (0, 1))
    got = fetched(chip, 2, (0, 1))
    stride = 2
    passed = swapped(mine[:TOP])
    mine = call(join_kernel, [(PART, NS)], which, got, mine, passed)
    while 2 * stride < chips:
        got = fetched(mine, stride, (0, 1))
        passed = swapped(mine[:TOP])
        mine = call(join_kernel, [(PART, NS)], which, got, mine, passed)
        stride *= 2
    tails = mine[LOW:]
    to_second, to_first = [
        lax.ppermute(tails, AXES, [(2 * (c + stride) + 1, 2 * c + k) for c in range(chips - stride)])
        for k in (1, 0)
    ]
    passed = swapped(mine)
    square = (NS, NS)
    gain0, rest0, gain1, rest1 = call(
        late_kernel, [square, wide, square, wide], which, mine, passed,
        late[0], late_held[0], late[1], late_held[1],
    )
    smooth_cov, smooth_mean = call(
        end_kernel, [(2, NS, NS), (2, NS)], None, to_second, to_first, gain0, rest0, gain1, rest1,
        far_out=(0,), scratch=[pltpu.VMEM((2, NS, NS), jnp.float32), pltpu.SemaphoreType.DMA((2,))],
    )
    return (smooth_mean, smooth_cov)


def solution(mesh):
    in_specs = (P(AXES, None), P(AXES, None, None), P(AXES, None, None), P())
    out_specs = (P(AXES, None), P(AXES, None, None))
    return jax.shard_map(local, mesh=mesh, in_specs=in_specs, out_specs=out_specs, check_vma=False)
```

```python
import jax
import jax.numpy as jnp
from jax import lax
from jax.experimental import pallas as pl
from jax.experimental.pallas import tpu as pltpu
from jax.sharding import PartitionSpec as P

AXES = ("grp", "dev")
EXTRA = 8

BASE = 16
HALF = 128


def dot(left, right):
    return jnp.dot(left, right, precision=lax.Precision.HIGHEST, preferred_element_type=jnp.float32)


def eliminated(tops, base):
    tiles = [[t[8 * i : 8 * i + 8] for i in range(BASE // 8)] for t in tops]
    lane = lax.broadcasted_iota(jnp.int32, (8, HALF), 1)
    sub = lax.broadcasted_iota(jnp.int32, (8, HALF), 0)

    def spread(row):
        return jnp.broadcast_to(row, (8, HALF))

    cols = [[[spread(t[:, base + j : base + j + 1]) for t in tiles[m]] for j in range(BASE)] for m in range(2)]
    for k in range(BASE):
        q, o = divmod(k, 8)
        here = lane == base + k
        unit = jnp.where(sub == o, 1.0, 0.0)
        for m in range(2):
            col, tile = cols[m], tiles[m]
            ratio = 1.0 / spread(col[k][q][o : o + 1])
            scaled = jnp.where(here, ratio, spread(tile[q][o : o + 1]) * ratio)
            down = list(col[k])
            down[q] = down[q] - unit
            for j in range(k + 1, BASE):
                f = spread(col[j][q][o : o + 1]) * ratio
                col[j] = [c - d * f for c, d in zip(col[j], down)]
            for i in range(BASE // 8):
                old = jnp.where(here, unit if i == q else 0.0, tile[i])
                tile[i] = old - down[i] * scaled
    return [jnp.concatenate(t, axis=0) for t in tiles]


def less_product(rows, base, inside, new):
    parts = []
    for i in range(BASE // 8):
        old = rows[8 * i : 8 * i + 8]
        terms = [
            jnp.broadcast_to(old[:, base + k : base + k + 1], (8, HALF)) * jnp.broadcast_to(new[k : k + 1], (8, HALF))
            for k in range(BASE)
        ]
        while len(terms) > 1:
            terms = [a + b for a, b in zip(terms[::2], terms[1::2])]
        parts.append(jnp.where(inside[:8], 0.0, old) - terms[0])
    return jnp.concatenate(parts, axis=0)


def half_inverse(pair):
    lane = lax.broadcasted_iota(jnp.int32, (BASE, HALF), 1)
    count = HALF // BASE
    pair = [[p[BASE * i : BASE * i + BASE] for i in range(count)] for p in pair]
    for j in range(count):
        rows = slice(BASE * j, BASE * j + BASE)
        inside = (lane >= BASE * j) & (lane < BASE * (j + 1))
        news = eliminated([p[j] for p in pair], BASE * j)
        for m in range(2):
            first = (j + 1) % count
            rest = [i for i in range(count) if i not in (j, first)]
            old = pair[m]
            new = [None] * count
            new[j] = news[m]
            new[first] = less_product(old[first], BASE * j, inside, news[m])
            tall = jnp.concatenate([old[i][:, rows] for i in rest], axis=0)
            tall = dot(tall, news[m])
            for n, i in enumerate(rest):
                new[i] = jnp.where(inside, 0.0, old[i]) - tall[BASE * n : BASE * n + BASE]
            pair[m] = new
    return [jnp.concatenate(p, axis=0) for p in pair]


def solved_pair(pred, moved):
    lo, hi = slice(0, HALF), slice(HALF, 2 * HALF)
    inv = half_inverse([p[lo, lo] for p in pred])
    wide, corner, out = [], [], []
    for m in range(2):
        wide.append(dot(inv[m], jnp.concatenate([pred[m][lo, hi], moved[m][lo]], axis=1)))
        corner.append(pred[m][hi, hi] - dot(pred[m][hi, lo], wide[m][:, :HALF]))
    inv = half_inverse(corner)
    for m in range(2):
        rest = moved[m][hi] - dot(pred[m][hi, lo], wide[m][:, HALF:])
        low = dot(inv[m], rest)
        top = wide[m][:, HALF:] - dot(wide[m][:, :HALF], low)
        out.append(jnp.concatenate([top, low], axis=0))
    return out


NS = 256
TOP = 192
LOW = NS - TOP
OFFSET = LOW + HALF
DIAG = OFFSET + 1
PART = OFFSET + EXTRA


def flipped(matrix):
    return jnp.swapaxes(matrix, -1, -2)


def halves(value):
    high = value.astype(jnp.bfloat16)
    return high, (value - high.astype(jnp.float32)).astype(jnp.bfloat16)


def three(left, right, dims):
    lh, ll = halves(left)
    rh, rl = halves(right)

    def one(a, b):
        return lax.dot_general(a, b, (dims, ((), ())), preferred_element_type=jnp.float32)

    return one(lh, rh) + (one(lh, rl) + one(ll, rh))


def mdot(left, right):
    return three(left, right, ((1,), (0,)))


def tdot(left, right):
    return three(left, right, ((0,), (0,)))


def row_col():
    return (
        lax.broadcasted_iota(jnp.int32, (HALF, HALF), 0),
        lax.broadcasted_iota(jnp.int32, (HALF, HALF), 1),
    )


def packed(upper, corner):
    r, c = row_col()
    both = jnp.where(r >= c, upper[:, :HALF], corner)
    diag = jnp.sum(jnp.where(r == c, corner, 0.0), axis=0, keepdims=True)
    return jnp.concatenate([upper[:, HALF:], both], axis=1), diag


def unpacked(half, diag):
    r, c = row_col()
    right, both = half[:, :HALF], half[:, HALF:]
    turned = both.T
    left = jnp.where(r >= c, both, turned)
    corner = jnp.where(r < c, both, jnp.where(r == c, diag, turned))
    return jnp.concatenate(
        [jnp.concatenate([left, right], axis=1), jnp.concatenate([right.T, corner], axis=1)], axis=0
    )


def sandwich(inner, gain):
    first = mdot(inner, gain)
    upper = tdot(gain[:, :HALF], first)
    corner = tdot(gain[:, HALF:], first[:, HALF:])
    return packed(upper, corner)


def diag_row(diag):
    return jnp.concatenate([diag, jnp.zeros((1, NS - HALF), jnp.float32)], axis=1)


def store_held(out, base, half, diag, offset):
    out[base : base + HALF] = half
    tail = jnp.concatenate(
        [offset, diag_row(diag), jnp.zeros((EXTRA - 2, NS), jnp.float32)], axis=0
    )
    out[base + HALF : base + HALF + EXTRA] = tail


def exact(left, right, dims):
    return lax.dot_general(
        left, right, (dims, ((), ())),
        precision=lax.Precision.HIGHEST, preferred_element_type=jnp.float32,
    )


def local_kernel(
    final, mean_in, cov_in, noise_in, step_in, both, turned1, held1, mean, cov, noise, step_at, done
):
    moves = [(step_in, step_at), (cov_in.at[0], cov.at[0]), (cov_in.at[1], cov.at[1])]
    moves += [(noise_in.at[0], noise.at[0]), (noise_in.at[1], noise.at[1]), (mean_in, mean)]
    copies = [pltpu.make_async_copy(a, b, done.at[i]) for i, (a, b) in enumerate(moves)]
    for copy in copies:
        copy.start()
    copies[0].wait()
    step = step_at[...]
    moved = []
    for m in range(2):
        copies[1 + m].wait()
        moved.append(dot(step, cov[m]))
    for copy in copies[3:]:
        copy.wait()
    pred = [exact(moved[m], step, ((1,), (1,))) + noise[m] for m in range(2)]
    gains = solved_pair(pred, moved)
    gains[1] = jnp.where(final[0] == 1, 0.0, gains[1])
    means = jnp.concatenate([mean[...], jnp.zeros((EXTRA - 2, NS), jnp.float32)], axis=0)
    ahead = exact(means, step, ((1,), (1,)))
    rests = [cov[m] - exact(gains[m], moved[m], ((0,), (0,))) for m in range(2)]
    offsets = [means - dot(ahead, gains[m]) for m in range(2)]
    turned1[...] = gains[1]
    held1[:NS] = rests[1]
    held1[NS:] = jnp.broadcast_to(offsets[1][1:2], (EXTRA, NS))
    both[:NS] = mdot(gains[1], gains[0])
    both[NS : 2 * NS] = tdot(gains[0], mdot(rests[1], gains[0])) + rests[0]
    second = mdot(offsets[1], gains[0])[1:2]
    both[2 * NS :] = jnp.broadcast_to(second + offsets[0][:1], (EXTRA, NS))


def chip_kernel(core, own, other, out):
    @pl.when(core[0] == 0)
    def _():
        out[:TOP] = mdot(other[:TOP], own[:NS])
        out[TOP:] = jnp.zeros((PART - TOP, NS), jnp.float32)

    @pl.when(core[0] == 1)
    def _():
        gain = other[:NS]
        out[:LOW] = mdot(own[TOP:NS], gain)
        half, diag = sandwich(own[NS : 2 * NS], gain)
        add, add_diag = packed(other[NS : NS + HALF], other[NS + HALF : 2 * NS, HALF:])
        tail = mdot(own[2 * NS :], gain) + other[2 * NS :]
        store_held(out, LOW, half + add, diag + add_diag, tail[:1])


def join_kernel(core, got, mine, passed, out):
    @pl.when(core[0] == 0)
    def _():
        gain = jnp.concatenate([mine[:TOP], passed[:LOW]], axis=0)
        out[:TOP] = mdot(got[:TOP], gain)
        out[TOP:] = jnp.zeros((PART - TOP, NS), jnp.float32)

    @pl.when(core[0] == 1)
    def _():
        gain = jnp.concatenate([passed[:TOP], mine[:LOW]], axis=0)
        out[:LOW] = mdot(got[:LOW], gain)
        inner = unpacked(got[LOW:OFFSET], got[DIAG : DIAG + 1, :HALF])
        half, diag = sandwich(inner, gain)
        tail = mdot(got[OFFSET:], gain)
        store_held(
            out, LOW, half + mine[LOW:OFFSET], diag + mine[DIAG : DIAG + 1, :HALF],
            tail[:1] + mine[OFFSET : OFFSET + 1],
        )


def late_kernel(core, mine, passed, turned0, held0, turned1, held1, gain0, rest0, gain1, rest1):
    first = core[0] == 0
    gain = jnp.where(
        first,
        jnp.concatenate([mine[:TOP], passed[:LOW]], axis=0),
        jnp.concatenate([passed[:TOP], mine[:LOW]], axis=0),
    )
    own = jnp.where(first, passed[LOW:], mine[LOW:])
    inner = unpacked(own[:HALF], own[HALF + 1 : HALF + 2, :HALF])
    for turned, held, full, rest in (
        (turned0[...], held0, gain0, rest0), (turned1[...], held1, gain1, rest1)
    ):
        full[...] = mdot(gain, turned)
        rest[:NS] = tdot(turned, mdot(inner, turned)) + held[:NS]
        rest[NS:] = mdot(own[HALF:], turned) + held[NS:]


def end_kernel(to_second, to_first, turned0, held0, turned1, held1, cov_out, mean, cov, done):
    after = to_second[...] + to_first[...]
    inner = unpacked(after[:HALF], after[HALF + 1 : HALF + 2, :HALF])
    copies = [pltpu.make_async_copy(cov.at[i], cov_out.at[i], done.at[i]) for i in range(2)]
    for i, (turned, held) in enumerate(((turned0, held0), (turned1, held1))):
        gain = turned[...]
        cov[i] = tdot(gain, mdot(inner, gain)) + held[:NS]
        copies[i].start()
        mean[i : i + 1] = (mdot(after[HALF:], gain) + held[NS:])[:1]
    for copy in copies:
        copy.wait()


def call(kernel, shapes, scalar, *arrays, far_in=False, far_out=(), scratch=()):
    vmem = pl.BlockSpec(memory_space=pltpu.VMEM)
    far = pl.BlockSpec(memory_space=pltpu.HBM)
    smem = pl.BlockSpec(memory_space=pltpu.SMEM)
    scalars = [] if scalar is None else [scalar]
    outs = [jax.ShapeDtypeStruct(s, jnp.float32) for s in shapes]
    done = pl.pallas_call(
        kernel,
        out_shape=outs,
        in_specs=[smem] * len(scalars) + [far if far_in else vmem] * len(arrays),
        out_specs=[far if i in far_out else vmem for i in range(len(outs))],
        scratch_shapes=scratch,
        compiler_params=pltpu.CompilerParams(vmem_limit_bytes=32 * 1024 * 1024),
    )(*scalars, *arrays)
    return done if len(outs) > 1 else done[0]


def product(left, right):
    return jnp.matmul(left, right, precision=lax.Precision.HIGHEST)


def applied(turned, held_next, held):
    width = turned.shape[0]
    first = product(held_next, turned)
    square = product(flipped(turned), first[:width]) + held[:width]
    return jnp.concatenate([square, first[width:] + held[width:]], axis=0)


def local(filt_mean, filt_cov, noise_cov, transition):
    devices = lax.axis_size(AXES)
    chips = devices // 2
    place = lax.axis_index(AXES)
    core = place % 2
    is_first = core == 0
    which = core.astype(jnp.int32)[None]
    final = (place == devices - 1).astype(jnp.int32)[None]
    wide = (NS + EXTRA, NS)
    both, turned1, held1 = call(
        local_kernel, [(2 * NS + EXTRA, NS), (NS, NS), wide], final,
        *(pltpu.with_memory_space_constraint(a, pltpu.HBM) for a in (filt_mean, filt_cov, noise_cov, transition)),
        far_in=True,
        scratch=[
            *(pltpu.VMEM(a.shape, jnp.float32) for a in (filt_mean, filt_cov, noise_cov, transition)),
            pltpu.SemaphoreType.DMA((6,)),
        ],
    )

    swap = [(p, p ^ 1) for p in range(devices)]

    def swapped(rows):
        return lax.ppermute(rows, AXES, swap)

    other = swapped(both)
    chip = call(chip_kernel, [(PART, NS)], which, both, other)
    both_turned, both_held = both[:NS], both[NS:]
    late = [jnp.where(is_first, product(other[:NS], t), t) for t in (both_turned, turned1)]
    late_held = [
        jnp.where(is_first, applied(t, other[NS:], h), h)
        for t, h in ((both_turned, both_held), (turned1, held1))
    ]

    def fetched(rows, stride, cores):
        return lax.ppermute(
            rows, AXES, [(2 * (c + stride) + k, 2 * c + k) for c in range(chips - stride) for k in cores]
        )

    got = fetched(chip, 2, (0, 1))
    nearer, late[1] = lax.optimization_barrier((chip, late[1]))
    mine = fetched(nearer, 1, (0, 1))
    stride = 2
    passed = swapped(mine[:TOP])
    mine = call(join_kernel, [(PART, NS)], which, got, mine, passed)
    while 2 * stride < chips:
        got = fetched(mine, stride, (0, 1))
        passed = swapped(mine[:TOP])
        mine = call(join_kernel, [(PART, NS)], which, got, mine, passed)
        stride *= 2
    tails = mine[LOW:]
    to_second, to_first = [
        lax.ppermute(tails, AXES, [(2 * (c + stride) + 1, 2 * c + k) for c in range(chips - stride)])
        for k in (1, 0)
    ]
    passed = swapped(mine)
    square = (NS, NS)
    gain0, rest0, gain1, rest1 = call(
        late_kernel, [square, wide, square, wide], which, mine, passed,
        late[0], late_held[0], late[1], late_held[1],
    )
    smooth_cov, smooth_mean = call(
        end_kernel, [(2, NS, NS), (2, NS)], None, to_second, to_first, gain0, rest0, gain1, rest1,
        far_out=(0,), scratch=[pltpu.VMEM((2, NS, NS), jnp.float32), pltpu.SemaphoreType.DMA((2,))],
    )
    return (smooth_mean, smooth_cov)


def solution(mesh):
    in_specs = (P(AXES, None), P(AXES, None, None), P(AXES, None, None), P())
    out_specs = (P(AXES, None), P(AXES, None, None))
    return jax.shard_map(local, mesh=mesh, in_specs=in_specs, out_specs=out_specs, check_vma=False)
```

```python
import jax
import jax.numpy as jnp
from jax import lax
from jax.experimental import pallas as pl
from jax.experimental.pallas import tpu as pltpu
from jax.sharding import PartitionSpec as P

AXES = ("grp", "dev")
EXTRA = 8

BASE = 16
HALF = 128


def dot(left, right):
    return jnp.dot(left, right, precision=lax.Precision.HIGHEST, preferred_element_type=jnp.float32)


def eliminated(tops, base):
    tiles = [[t[8 * i : 8 * i + 8] for i in range(BASE // 8)] for t in tops]
    lane = lax.broadcasted_iota(jnp.int32, (8, HALF), 1)
    sub = lax.broadcasted_iota(jnp.int32, (8, HALF), 0)

    def spread(row):
        return jnp.broadcast_to(row, (8, HALF))

    cols = [[[spread(t[:, base + j : base + j + 1]) for t in tiles[m]] for j in range(BASE)] for m in range(2)]
    for k in range(BASE):
        q, o = divmod(k, 8)
        here = lane == base + k
        unit = jnp.where(sub == o, 1.0, 0.0)
        for m in range(2):
            col, tile = cols[m], tiles[m]
            ratio = 1.0 / spread(col[k][q][o : o + 1])
            scaled = jnp.where(here, ratio, spread(tile[q][o : o + 1]) * ratio)
            down = list(col[k])
            down[q] = down[q] - unit
            for j in range(k + 1, BASE):
                f = spread(col[j][q][o : o + 1]) * ratio
                col[j] = [c - d * f for c, d in zip(col[j], down)]
            for i in range(BASE // 8):
                old = jnp.where(here, unit if i == q else 0.0, tile[i])
                tile[i] = old - down[i] * scaled
    return [jnp.concatenate(t, axis=0) for t in tiles]


def less_product(rows, base, inside, new):
    parts = []
    for i in range(BASE // 8):
        old = rows[8 * i : 8 * i + 8]
        terms = [
            jnp.broadcast_to(old[:, base + k : base + k + 1], (8, HALF)) * jnp.broadcast_to(new[k : k + 1], (8, HALF))
            for k in range(BASE)
        ]
        while len(terms) > 1:
            terms = [a + b for a, b in zip(terms[::2], terms[1::2])]
        parts.append(jnp.where(inside[:8], 0.0, old) - terms[0])
    return jnp.concatenate(parts, axis=0)


def half_inverse(pair):
    lane = lax.broadcasted_iota(jnp.int32, (BASE, HALF), 1)
    count = HALF // BASE
    pair = [[p[BASE * i : BASE * i + BASE] for i in range(count)] for p in pair]
    for j in range(count):
        rows = slice(BASE * j, BASE * j + BASE)
        inside = (lane >= BASE * j) & (lane < BASE * (j + 1))
        news = eliminated([p[j] for p in pair], BASE * j)
        for m in range(2):
            first = (j + 1) % count
            rest = [i for i in range(count) if i not in (j, first)]
            old = pair[m]
            new = [None] * count
            new[j] = news[m]
            new[first] = less_product(old[first], BASE * j, inside, news[m])
            tall = jnp.concatenate([old[i][:, rows] for i in rest], axis=0)
            tall = dot(tall, news[m])
            for n, i in enumerate(rest):
                new[i] = jnp.where(inside, 0.0, old[i]) - tall[BASE * n : BASE * n + BASE]
            pair[m] = new
    return [jnp.concatenate(p, axis=0) for p in pair]


def solved_pair(pred, moved):
    lo, hi = slice(0, HALF), slice(HALF, 2 * HALF)
    inv = half_inverse([p[lo, lo] for p in pred])
    wide, corner, out = [], [], []
    for m in range(2):
        wide.append(dot(inv[m], jnp.concatenate([pred[m][lo, hi], moved[m][lo]], axis=1)))
        corner.append(pred[m][hi, hi] - dot(pred[m][hi, lo], wide[m][:, :HALF]))
    inv = half_inverse(corner)
    for m in range(2):
        rest = moved[m][hi] - dot(pred[m][hi, lo], wide[m][:, HALF:])
        low = dot(inv[m], rest)
        top = wide[m][:, HALF:] - dot(wide[m][:, :HALF], low)
        out.append(jnp.concatenate([top, low], axis=0))
    return out


NS = 256
TOP = 192
LOW = NS - TOP
OFFSET = LOW + HALF
DIAG = OFFSET + 1
PART = OFFSET + EXTRA


def flipped(matrix):
    return jnp.swapaxes(matrix, -1, -2)


def halves(value):
    high = value.astype(jnp.bfloat16)
    return high, (value - high.astype(jnp.float32)).astype(jnp.bfloat16)


def three(left, right, dims):
    lh, ll = halves(left)
    rh, rl = halves(right)

    def one(a, b):
        return lax.dot_general(a, b, (dims, ((), ())), preferred_element_type=jnp.float32)

    return one(lh, rh) + (one(lh, rl) + one(ll, rh))


def mdot(left, right):
    return three(left, right, ((1,), (0,)))


def tdot(left, right):
    return three(left, right, ((0,), (0,)))


def row_col():
    return (
        lax.broadcasted_iota(jnp.int32, (HALF, HALF), 0),
        lax.broadcasted_iota(jnp.int32, (HALF, HALF), 1),
    )


def packed(upper, corner):
    r, c = row_col()
    both = jnp.where(r >= c, upper[:, :HALF], corner)
    diag = jnp.sum(jnp.where(r == c, corner, 0.0), axis=0, keepdims=True)
    return jnp.concatenate([upper[:, HALF:], both], axis=1), diag


def unpacked(half, diag):
    r, c = row_col()
    right, both = half[:, :HALF], half[:, HALF:]
    turned = both.T
    left = jnp.where(r >= c, both, turned)
    corner = jnp.where(r < c, both, jnp.where(r == c, diag, turned))
    return jnp.concatenate(
        [jnp.concatenate([left, right], axis=1), jnp.concatenate([right.T, corner], axis=1)], axis=0
    )


def sandwich(inner, gain):
    first = mdot(inner, gain)
    upper = tdot(gain[:, :HALF], first)
    corner = tdot(gain[:, HALF:], first[:, HALF:])
    return packed(upper, corner)


def diag_row(diag):
    return jnp.concatenate([diag, jnp.zeros((1, NS - HALF), jnp.float32)], axis=1)


def store_held(out, base, half, diag, offset):
    out[base : base + HALF] = half
    tail = jnp.concatenate(
        [offset, diag_row(diag), jnp.zeros((EXTRA - 2, NS), jnp.float32)], axis=0
    )
    out[base + HALF : base + HALF + EXTRA] = tail


def exact(left, right, dims):
    return lax.dot_general(
        left, right, (dims, ((), ())),
        precision=lax.Precision.HIGHEST, preferred_element_type=jnp.float32,
    )


def local_kernel(
    final, mean_in, cov_in, noise_in, step_in, both, turned1, held1, mean, cov, noise, step_at, done
):
    moves = [(step_in, step_at), (cov_in.at[0], cov.at[0]), (cov_in.at[1], cov.at[1])]
    moves += [(noise_in.at[0], noise.at[0]), (noise_in.at[1], noise.at[1]), (mean_in, mean)]
    copies = [pltpu.make_async_copy(a, b, done.at[i]) for i, (a, b) in enumerate(moves)]
    for copy in copies:
        copy.start()
    copies[0].wait()
    step = step_at[...]
    moved = []
    for m in range(2):
        copies[1 + m].wait()
        moved.append(dot(step, cov[m]))
    for copy in copies[3:]:
        copy.wait()
    pred = [exact(moved[m], step, ((1,), (1,))) + noise[m] for m in range(2)]
    gains = solved_pair(pred, moved)
    gains[1] = jnp.where(final[0] == 1, 0.0, gains[1])
    means = jnp.concatenate([mean[...], jnp.zeros((EXTRA - 2, NS), jnp.float32)], axis=0)
    ahead = exact(means, step, ((1,), (1,)))
    rests = [cov[m] - exact(gains[m], moved[m], ((0,), (0,))) for m in range(2)]
    offsets = [means - dot(ahead, gains[m]) for m in range(2)]
    turned1[...] = gains[1]
    held1[:NS] = rests[1]
    held1[NS:] = jnp.broadcast_to(offsets[1][1:2], (EXTRA, NS))
    both[:NS] = mdot(gains[1], gains[0])
    both[NS : 2 * NS] = tdot(gains[0], mdot(rests[1], gains[0])) + rests[0]
    second = mdot(offsets[1], gains[0])[1:2]
    both[2 * NS :] = jnp.broadcast_to(second + offsets[0][:1], (EXTRA, NS))


def chip_kernel(core, own, other, out):
    @pl.when(core[0] == 0)
    def _():
        out[:TOP] = mdot(other[:TOP], own[:NS])
        out[TOP:] = jnp.zeros((PART - TOP, NS), jnp.float32)

    @pl.when(core[0] == 1)
    def _():
        gain = other[:NS]
        out[:LOW] = mdot(own[TOP:NS], gain)
        half, diag = sandwich(own[NS : 2 * NS], gain)
        add, add_diag = packed(other[NS : NS + HALF], other[NS + HALF : 2 * NS, HALF:])
        tail = mdot(own[2 * NS :], gain) + other[2 * NS :]
        store_held(out, LOW, half + add, diag + add_diag, tail[:1])


def join_kernel(core, got, mine, passed, out):
    @pl.when(core[0] == 0)
    def _():
        gain = jnp.concatenate([mine[:TOP], passed[:LOW]], axis=0)
        out[:TOP] = mdot(got[:TOP], gain)
        out[TOP:] = jnp.zeros((PART - TOP, NS), jnp.float32)

    @pl.when(core[0] == 1)
    def _():
        gain = jnp.concatenate([passed[:TOP], mine[:LOW]], axis=0)
        out[:LOW] = mdot(got[:LOW], gain)
        inner = unpacked(got[LOW:OFFSET], got[DIAG : DIAG + 1, :HALF])
        half, diag = sandwich(inner, gain)
        tail = mdot(got[OFFSET:], gain)
        store_held(
            out, LOW, half + mine[LOW:OFFSET], diag + mine[DIAG : DIAG + 1, :HALF],
            tail[:1] + mine[OFFSET : OFFSET + 1],
        )


def late_kernel(core, mine, passed, turned0, held0, turned1, held1, gain0, rest0, gain1, rest1):
    first = core[0] == 0
    gain = jnp.where(
        first,
        jnp.concatenate([mine[:TOP], passed[:LOW]], axis=0),
        jnp.concatenate([passed[:TOP], mine[:LOW]], axis=0),
    )
    own = jnp.where(first, passed[LOW:], mine[LOW:])
    inner = unpacked(own[:HALF], own[HALF + 1 : HALF + 2, :HALF])
    for turned, held, full, rest in (
        (turned0[...], held0, gain0, rest0), (turned1[...], held1, gain1, rest1)
    ):
        full[...] = mdot(gain, turned)
        rest[:NS] = tdot(turned, mdot(inner, turned)) + held[:NS]
        rest[NS:] = mdot(own[HALF:], turned) + held[NS:]


def end_kernel(to_second, to_first, turned0, held0, turned1, held1, cov, mean):
    after = to_second[...] + to_first[...]
    inner = unpacked(after[:HALF], after[HALF + 1 : HALF + 2, :HALF])
    for i, (turned, held) in enumerate(((turned0, held0), (turned1, held1))):
        gain = turned[...]
        cov[i] = tdot(gain, mdot(inner, gain)) + held[:NS]
        mean[i : i + 1] = (mdot(after[HALF:], gain) + held[NS:])[:1]


def call(kernel, shapes, scalar, *arrays, far_in=False, scratch=()):
    vmem = pl.BlockSpec(memory_space=pltpu.VMEM)
    far = pl.BlockSpec(memory_space=pltpu.HBM)
    smem = pl.BlockSpec(memory_space=pltpu.SMEM)
    scalars = [] if scalar is None else [scalar]
    outs = [jax.ShapeDtypeStruct(s, jnp.float32) for s in shapes]
    done = pl.pallas_call(
        kernel,
        out_shape=outs,
        in_specs=[smem] * len(scalars) + [far if far_in else vmem] * len(arrays),
        out_specs=[vmem] * len(outs),
        scratch_shapes=scratch,
        compiler_params=pltpu.CompilerParams(vmem_limit_bytes=32 * 1024 * 1024),
    )(*scalars, *arrays)
    return done if len(outs) > 1 else done[0]


def product(left, right):
    return jnp.matmul(left, right, precision=lax.Precision.HIGHEST)


def applied(turned, held_next, held):
    width = turned.shape[0]
    first = product(held_next, turned)
    square = product(flipped(turned), first[:width]) + held[:width]
    return jnp.concatenate([square, first[width:] + held[width:]], axis=0)


def local(filt_mean, filt_cov, noise_cov, transition):
    devices = lax.axis_size(AXES)
    chips = devices // 2
    place = lax.axis_index(AXES)
    core = place % 2
    is_first = core == 0
    which = core.astype(jnp.int32)[None]
    final = (place == devices - 1).astype(jnp.int32)[None]
    wide = (NS + EXTRA, NS)
    both, turned1, held1 = call(
        local_kernel, [(2 * NS + EXTRA, NS), (NS, NS), wide], final,
        *(pltpu.with_memory_space_constraint(a, pltpu.HBM) for a in (filt_mean, filt_cov, noise_cov, transition)),
        far_in=True,
        scratch=[
            *(pltpu.VMEM(a.shape, jnp.float32) for a in (filt_mean, filt_cov, noise_cov, transition)),
            pltpu.SemaphoreType.DMA((6,)),
        ],
    )

    swap = [(p, p ^ 1) for p in range(devices)]

    def swapped(rows):
        return lax.ppermute(rows, AXES, swap)

    other = swapped(both)
    chip = call(chip_kernel, [(PART, NS)], which, both, other)
    both_turned, both_held = both[:NS], both[NS:]
    late = [jnp.where(is_first, product(other[:NS], t), t) for t in (both_turned, turned1)]
    late_held = [
        jnp.where(is_first, applied(t, other[NS:], h), h)
        for t, h in ((both_turned, both_held), (turned1, held1))
    ]

    def fetched(rows, stride, cores):
        return lax.ppermute(
            rows, AXES, [(2 * (c + stride) + k, 2 * c + k) for c in range(chips - stride) for k in cores]
        )

    got = fetched(chip, 1, (0, 1))
    passed = swapped(chip[:TOP])
    mine = call(join_kernel, [(PART, NS)], which, got, chip, passed)
    got = fetched(mine, 3, (0, 1))
    mine = fetched(mine, 1, (0, 1))
    passed = swapped(mine[:TOP])
    mine = call(join_kernel, [(PART, NS)], which, got, mine, passed)
    stride = 4
    while 2 * stride < chips:
        got = fetched(mine, stride, (0, 1))
        passed = swapped(mine[:TOP])
        mine = call(join_kernel, [(PART, NS)], which, got, mine, passed)
        stride *= 2
    tails = mine[LOW:]
    to_second, to_first = [
        lax.ppermute(tails, AXES, [(2 * (c + stride) + 1, 2 * c + k) for c in range(chips - stride)])
        for k in (1, 0)
    ]
    passed = swapped(mine)
    square = (NS, NS)
    gain0, rest0, gain1, rest1 = call(
        late_kernel, [square, wide, square, wide], which, mine, passed,
        late[0], late_held[0], late[1], late_held[1],
    )
    smooth_cov, smooth_mean = call(
        end_kernel, [(2, NS, NS), (2, NS)], None, to_second, to_first, gain0, rest0, gain1, rest1
    )
    return (smooth_mean, smooth_cov)


def solution(mesh):
    in_specs = (P(AXES, None), P(AXES, None, None), P(AXES, None, None), P())
    out_specs = (P(AXES, None), P(AXES, None, None))
    return jax.shard_map(local, mesh=mesh, in_specs=in_specs, out_specs=out_specs, check_vma=False)
```

```python
import jax
import jax.numpy as jnp
from jax import lax
from jax.experimental import pallas as pl
from jax.experimental.pallas import tpu as pltpu
from jax.sharding import PartitionSpec as P

AXES = ("grp", "dev")
EXTRA = 8

BASE = 16
HALF = 128


def dot(left, right):
    return jnp.dot(left, right, precision=lax.Precision.HIGHEST, preferred_element_type=jnp.float32)


def eliminated(tops, base):
    tiles = [[t[8 * i : 8 * i + 8] for i in range(BASE // 8)] for t in tops]
    lane = lax.broadcasted_iota(jnp.int32, (8, HALF), 1)
    sub = lax.broadcasted_iota(jnp.int32, (8, HALF), 0)

    def spread(row):
        return jnp.broadcast_to(row, (8, HALF))

    cols = [[[spread(t[:, base + j : base + j + 1]) for t in tiles[m]] for j in range(BASE)] for m in range(2)]
    for k in range(BASE):
        q, o = divmod(k, 8)
        here = lane == base + k
        unit = jnp.where(sub == o, 1.0, 0.0)
        for m in range(2):
            col, tile = cols[m], tiles[m]
            ratio = 1.0 / spread(col[k][q][o : o + 1])
            scaled = jnp.where(here, ratio, spread(tile[q][o : o + 1]) * ratio)
            down = list(col[k])
            down[q] = down[q] - unit
            for j in range(k + 1, BASE):
                f = spread(col[j][q][o : o + 1]) * ratio
                col[j] = [c - d * f for c, d in zip(col[j], down)]
            for i in range(BASE // 8):
                old = jnp.where(here, unit if i == q else 0.0, tile[i])
                tile[i] = old - down[i] * scaled
    return [jnp.concatenate(t, axis=0) for t in tiles]


def less_product(rows, base, inside, new):
    parts = []
    for i in range(BASE // 8):
        old = rows[8 * i : 8 * i + 8]
        terms = [
            jnp.broadcast_to(old[:, base + k : base + k + 1], (8, HALF)) * jnp.broadcast_to(new[k : k + 1], (8, HALF))
            for k in range(BASE)
        ]
        while len(terms) > 1:
            terms = [a + b for a, b in zip(terms[::2], terms[1::2])]
        parts.append(jnp.where(inside[:8], 0.0, old) - terms[0])
    return jnp.concatenate(parts, axis=0)


def half_inverse(pair):
    lane = lax.broadcasted_iota(jnp.int32, (BASE, HALF), 1)
    count = HALF // BASE
    pair = [[p[BASE * i : BASE * i + BASE] for i in range(count)] for p in pair]
    for j in range(count):
        rows = slice(BASE * j, BASE * j + BASE)
        inside = (lane >= BASE * j) & (lane < BASE * (j + 1))
        news = eliminated([p[j] for p in pair], BASE * j)
        for m in range(2):
            first = (j + 1) % count
            rest = [i for i in range(count) if i not in (j, first)]
            old = pair[m]
            new = [None] * count
            new[j] = news[m]
            new[first] = less_product(old[first], BASE * j, inside, news[m])
            tall = jnp.concatenate([old[i][:, rows] for i in rest], axis=0)
            tall = dot(tall, news[m])
            for n, i in enumerate(rest):
                new[i] = jnp.where(inside, 0.0, old[i]) - tall[BASE * n : BASE * n + BASE]
            pair[m] = new
    return [jnp.concatenate(p, axis=0) for p in pair]


def solved_pair(pred, moved):
    lo, hi = slice(0, HALF), slice(HALF, 2 * HALF)
    inv = half_inverse([p[lo, lo] for p in pred])
    wide, corner, out = [], [], []
    for m in range(2):
        wide.append(dot(inv[m], jnp.concatenate([pred[m][lo, hi], moved[m][lo]], axis=1)))
        corner.append(pred[m][hi, hi] - dot(pred[m][hi, lo], wide[m][:, :HALF]))
    inv = half_inverse(corner)
    for m in range(2):
        rest = moved[m][hi] - dot(pred[m][hi, lo], wide[m][:, HALF:])
        low = dot(inv[m], rest)
        top = wide[m][:, HALF:] - dot(wide[m][:, :HALF], low)
        out.append(jnp.concatenate([top, low], axis=0))
    return out


NS = 256
TOP = 192
LOW = NS - TOP
OFFSET = LOW + HALF
DIAG = OFFSET + 1
PART = OFFSET + EXTRA


def flipped(matrix):
    return jnp.swapaxes(matrix, -1, -2)


def halves(value):
    high = value.astype(jnp.bfloat16)
    return high, (value - high.astype(jnp.float32)).astype(jnp.bfloat16)


def three(left, right, dims):
    lh, ll = halves(left)
    rh, rl = halves(right)

    def one(a, b):
        return lax.dot_general(a, b, (dims, ((), ())), preferred_element_type=jnp.float32)

    return one(lh, rh) + (one(lh, rl) + one(ll, rh))


def mdot(left, right):
    return three(left, right, ((1,), (0,)))


def tdot(left, right):
    return three(left, right, ((0,), (0,)))


def row_col():
    return (
        lax.broadcasted_iota(jnp.int32, (HALF, HALF), 0),
        lax.broadcasted_iota(jnp.int32, (HALF, HALF), 1),
    )


def packed(upper, corner):
    r, c = row_col()
    both = jnp.where(r >= c, upper[:, :HALF], corner)
    diag = jnp.sum(jnp.where(r == c, corner, 0.0), axis=0, keepdims=True)
    return jnp.concatenate([upper[:, HALF:], both], axis=1), diag


def unpacked(half, diag):
    r, c = row_col()
    right, both = half[:, :HALF], half[:, HALF:]
    turned = both.T
    left = jnp.where(r >= c, both, turned)
    corner = jnp.where(r < c, both, jnp.where(r == c, diag, turned))
    return jnp.concatenate(
        [jnp.concatenate([left, right], axis=1), jnp.concatenate([right.T, corner], axis=1)], axis=0
    )


def sandwich(inner, gain):
    first = mdot(inner, gain)
    upper = tdot(gain[:, :HALF], first)
    corner = tdot(gain[:, HALF:], first[:, HALF:])
    return packed(upper, corner)


def diag_row(diag):
    return jnp.concatenate([diag, jnp.zeros((1, NS - HALF), jnp.float32)], axis=1)


def store_held(out, base, half, diag, offset):
    out[base : base + HALF] = half
    tail = jnp.concatenate(
        [offset, diag_row(diag), jnp.zeros((EXTRA - 2, NS), jnp.float32)], axis=0
    )
    out[base + HALF : base + HALF + EXTRA] = tail


def exact(left, right, dims):
    return lax.dot_general(
        left, right, (dims, ((), ())),
        precision=lax.Precision.HIGHEST, preferred_element_type=jnp.float32,
    )


def local_kernel(
    final, mean_in, cov_in, noise_in, step_in, both, turned1, held1, mean, cov, noise, step_at, done
):
    moves = [(step_in, step_at), (cov_in.at[0], cov.at[0]), (cov_in.at[1], cov.at[1])]
    moves += [(noise_in.at[0], noise.at[0]), (noise_in.at[1], noise.at[1]), (mean_in, mean)]
    copies = [pltpu.make_async_copy(a, b, done.at[i]) for i, (a, b) in enumerate(moves)]
    for copy in copies:
        copy.start()
    copies[0].wait()
    step = step_at[...]
    moved = []
    for m in range(2):
        copies[1 + m].wait()
        moved.append(dot(step, cov[m]))
    for copy in copies[3:]:
        copy.wait()
    pred = [exact(moved[m], step, ((1,), (1,))) + noise[m] for m in range(2)]
    gains = solved_pair(pred, moved)
    gains[1] = jnp.where(final[0] == 1, 0.0, gains[1])
    means = jnp.concatenate([mean[...], jnp.zeros((EXTRA - 2, NS), jnp.float32)], axis=0)
    ahead = exact(means, step, ((1,), (1,)))
    rests = [cov[m] - exact(gains[m], moved[m], ((0,), (0,))) for m in range(2)]
    offsets = [means - dot(ahead, gains[m]) for m in range(2)]
    turned1[...] = gains[1]
    held1[:NS] = rests[1]
    held1[NS:] = jnp.broadcast_to(offsets[1][1:2], (EXTRA, NS))
    both[:NS] = mdot(gains[1], gains[0])
    both[NS : 2 * NS] = tdot(gains[0], mdot(rests[1], gains[0])) + rests[0]
    second = mdot(offsets[1], gains[0])[1:2]
    both[2 * NS :] = jnp.broadcast_to(second + offsets[0][:1], (EXTRA, NS))


def chip_kernel(core, own, other, out):
    @pl.when(core[0] == 0)
    def _():
        out[:TOP] = mdot(other[:TOP], own[:NS])
        out[TOP:] = jnp.zeros((PART - TOP, NS), jnp.float32)

    @pl.when(core[0] == 1)
    def _():
        gain = other[:NS]
        out[:LOW] = mdot(own[TOP:NS], gain)
        half, diag = sandwich(own[NS : 2 * NS], gain)
        add, add_diag = packed(other[NS : NS + HALF], other[NS + HALF : 2 * NS, HALF:])
        tail = mdot(own[2 * NS :], gain) + other[2 * NS :]
        store_held(out, LOW, half + add, diag + add_diag, tail[:1])


def join_kernel(core, got, mine, passed, out):
    @pl.when(core[0] == 0)
    def _():
        gain = jnp.concatenate([mine[:TOP], passed[:LOW]], axis=0)
        out[:TOP] = mdot(got[:TOP], gain)
        out[TOP:] = jnp.zeros((PART - TOP, NS), jnp.float32)

    @pl.when(core[0] == 1)
    def _():
        gain = jnp.concatenate([passed[:TOP], mine[:LOW]], axis=0)
        out[:LOW] = mdot(got[:LOW], gain)
        inner = unpacked(got[LOW:OFFSET], got[DIAG : DIAG + 1, :HALF])
        half, diag = sandwich(inner, gain)
        tail = mdot(got[OFFSET:], gain)
        store_held(
            out, LOW, half + mine[LOW:OFFSET], diag + mine[DIAG : DIAG + 1, :HALF],
            tail[:1] + mine[OFFSET : OFFSET + 1],
        )


def late_kernel(core, mine, passed, turned0, held0, turned1, held1, gain0, rest0, gain1, rest1):
    first = core[0] == 0
    gain = jnp.where(
        first,
        jnp.concatenate([mine[:TOP], passed[:LOW]], axis=0),
        jnp.concatenate([passed[:TOP], mine[:LOW]], axis=0),
    )
    own = jnp.where(first, passed[LOW:], mine[LOW:])
    inner = unpacked(own[:HALF], own[HALF + 1 : HALF + 2, :HALF])
    for turned, held, full, rest in (
        (turned0[...], held0, gain0, rest0), (turned1[...], held1, gain1, rest1)
    ):
        full[...] = mdot(gain, turned)
        rest[:NS] = tdot(turned, mdot(inner, turned)) + held[:NS]
        rest[NS:] = mdot(own[HALF:], turned) + held[NS:]


def end_kernel(to_second, to_first, turned0, held0, turned1, held1, cov, mean):
    after = to_second[...] + to_first[...]
    inner = unpacked(after[:HALF], after[HALF + 1 : HALF + 2, :HALF])
    for i, (turned, held) in enumerate(((turned0, held0), (turned1, held1))):
        gain = turned[...]
        cov[i] = tdot(gain, mdot(inner, gain)) + held[:NS]
        mean[i : i + 1] = (mdot(after[HALF:], gain) + held[NS:])[:1]


def call(kernel, shapes, scalar, *arrays, far_in=False, scratch=()):
    vmem = pl.BlockSpec(memory_space=pltpu.VMEM)
    far = pl.BlockSpec(memory_space=pltpu.HBM)
    smem = pl.BlockSpec(memory_space=pltpu.SMEM)
    scalars = [] if scalar is None else [scalar]
    outs = [jax.ShapeDtypeStruct(s, jnp.float32) for s in shapes]
    done = pl.pallas_call(
        kernel,
        out_shape=outs,
        in_specs=[smem] * len(scalars) + [far if far_in else vmem] * len(arrays),
        out_specs=[vmem] * len(outs),
        scratch_shapes=scratch,
        compiler_params=pltpu.CompilerParams(vmem_limit_bytes=32 * 1024 * 1024),
    )(*scalars, *arrays)
    return done if len(outs) > 1 else done[0]


def product(left, right):
    return jnp.matmul(left, right, precision=lax.Precision.HIGHEST)


def applied(turned, held_next, held):
    width = turned.shape[0]
    first = product(held_next, turned)
    square = product(flipped(turned), first[:width]) + held[:width]
    return jnp.concatenate([square, first[width:] + held[width:]], axis=0)


def local(filt_mean, filt_cov, noise_cov, transition):
    devices = lax.axis_size(AXES)
    chips = devices // 2
    place = lax.axis_index(AXES)
    core = place % 2
    is_first = core == 0
    which = core.astype(jnp.int32)[None]
    final = (place == devices - 1).astype(jnp.int32)[None]
    wide = (NS + EXTRA, NS)
    both, turned1, held1 = call(
        local_kernel, [(2 * NS + EXTRA, NS), (NS, NS), wide], final,
        *(pltpu.with_memory_space_constraint(a, pltpu.HBM) for a in (filt_mean, filt_cov, noise_cov, transition)),
        far_in=True,
        scratch=[
            *(pltpu.VMEM(a.shape, jnp.float32) for a in (filt_mean, filt_cov, noise_cov, transition)),
            pltpu.SemaphoreType.DMA((6,)),
        ],
    )

    swap = [(p, p ^ 1) for p in range(devices)]

    def swapped(rows):
        return lax.ppermute(rows, AXES, swap)

    other = swapped(both)
    chip = call(chip_kernel, [(PART, NS)], which, both, other)
    both_turned, both_held = both[:NS], both[NS:]
    late = [jnp.where(is_first, product(other[:NS], t), t) for t in (both_turned, turned1)]
    late_held = [
        jnp.where(is_first, applied(t, other[NS:], h), h)
        for t, h in ((both_turned, both_held), (turned1, held1))
    ]

    def fetched(rows, stride, cores):
        return lax.ppermute(
            rows, AXES, [(2 * (c + stride) + k, 2 * c + k) for c in range(chips - stride) for k in cores]
        )

    mine = fetched(chip, 1, (0, 1))
    got = fetched(chip, 2, (0, 1))
    stride = 2
    passed = swapped(mine[:TOP])
    mine = call(join_kernel, [(PART, NS)], which, got, mine, passed)
    while 2 * stride < chips:
        got = fetched(mine, stride, (0, 1))
        passed = swapped(mine[:TOP])
        mine = call(join_kernel, [(PART, NS)], which, got, mine, passed)
        stride *= 2
    tails = mine[LOW:]
    to_second, to_first = [
        lax.ppermute(tails, AXES, [(2 * (c + stride) + 1, 2 * c + k) for c in range(chips - stride)])
        for k in (1, 0)
    ]
    passed = swapped(mine)
    square = (NS, NS)
    gain0, rest0, gain1, rest1 = call(
        late_kernel, [square, wide, square, wide], which, mine, passed,
        late[0], late_held[0], late[1], late_held[1],
    )
    smooth_cov, smooth_mean = call(
        end_kernel, [(2, NS, NS), (2, NS)], None, to_second, to_first, gain0, rest0, gain1, rest1
    )
    return (smooth_mean, smooth_cov)


def solution(mesh):
    in_specs = (P(AXES, None), P(AXES, None, None), P(AXES, None, None), P())
    out_specs = (P(AXES, None), P(AXES, None, None))
    return jax.shard_map(local, mesh=mesh, in_specs=in_specs, out_specs=out_specs, check_vma=False)
```

```python
import jax
import jax.numpy as jnp
from jax import lax
from jax.experimental import pallas as pl
from jax.experimental.pallas import tpu as pltpu
from jax.sharding import PartitionSpec as P

AXES = ("grp", "dev")
EXTRA = 8

BASE = 16
HALF = 128


def dot(left, right):
    return jnp.dot(left, right, precision=lax.Precision.HIGHEST, preferred_element_type=jnp.float32)


def eliminated(tops, base):
    tiles = [[t[8 * i : 8 * i + 8] for i in range(BASE // 8)] for t in tops]
    lane = lax.broadcasted_iota(jnp.int32, (8, HALF), 1)
    sub = lax.broadcasted_iota(jnp.int32, (8, HALF), 0)

    def spread(row):
        return jnp.broadcast_to(row, (8, HALF))

    cols = [[[spread(t[:, base + j : base + j + 1]) for t in tiles[m]] for j in range(BASE)] for m in range(2)]
    for k in range(BASE):
        q, o = divmod(k, 8)
        here = lane == base + k
        unit = jnp.where(sub == o, 1.0, 0.0)
        for m in range(2):
            col, tile = cols[m], tiles[m]
            ratio = 1.0 / spread(col[k][q][o : o + 1])
            scaled = jnp.where(here, ratio, spread(tile[q][o : o + 1]) * ratio)
            down = list(col[k])
            down[q] = down[q] - unit
            for j in range(k + 1, BASE):
                f = spread(col[j][q][o : o + 1]) * ratio
                col[j] = [c - d * f for c, d in zip(col[j], down)]
            for i in range(BASE // 8):
                old = jnp.where(here, unit if i == q else 0.0, tile[i])
                tile[i] = old - down[i] * scaled
    return [jnp.concatenate(t, axis=0) for t in tiles]


def less_product(rows, base, inside, new):
    parts = []
    for i in range(BASE // 8):
        old = rows[8 * i : 8 * i + 8]
        terms = [
            jnp.broadcast_to(old[:, base + k : base + k + 1], (8, HALF)) * jnp.broadcast_to(new[k : k + 1], (8, HALF))
            for k in range(BASE)
        ]
        while len(terms) > 1:
            terms = [a + b for a, b in zip(terms[::2], terms[1::2])]
        parts.append(jnp.where(inside[:8], 0.0, old) - terms[0])
    return jnp.concatenate(parts, axis=0)


def half_inverse(pair):
    lane = lax.broadcasted_iota(jnp.int32, (BASE, HALF), 1)
    count = HALF // BASE
    pair = [[p[BASE * i : BASE * i + BASE] for i in range(count)] for p in pair]
    for j in range(count):
        rows = slice(BASE * j, BASE * j + BASE)
        inside = (lane >= BASE * j) & (lane < BASE * (j + 1))
        news = eliminated([p[j] for p in pair], BASE * j)
        for m in range(2):
            first = (j + 1) % count
            rest = [i for i in range(count) if i not in (j, first)]
            old = pair[m]
            new = [None] * count
            new[j] = news[m]
            new[first] = less_product(old[first], BASE * j, inside, news[m])
            tall = jnp.concatenate([old[i][:, rows] for i in rest], axis=0)
            tall = dot(tall, news[m])
            for n, i in enumerate(rest):
                new[i] = jnp.where(inside, 0.0, old[i]) - tall[BASE * n : BASE * n + BASE]
            pair[m] = new
    return [jnp.concatenate(p, axis=0) for p in pair]


def solved_pair(pred, moved):
    lo, hi = slice(0, HALF), slice(HALF, 2 * HALF)
    inv = half_inverse([p[lo, lo] for p in pred])
    wide, corner, out = [], [], []
    for m in range(2):
        wide.append(dot(inv[m], jnp.concatenate([pred[m][lo, hi], moved[m][lo]], axis=1)))
        corner.append(pred[m][hi, hi] - dot(pred[m][hi, lo], wide[m][:, :HALF]))
    inv = half_inverse(corner)
    for m in range(2):
        rest = moved[m][hi] - dot(pred[m][hi, lo], wide[m][:, HALF:])
        low = dot(inv[m], rest)
        top = wide[m][:, HALF:] - dot(wide[m][:, :HALF], low)
        out.append(jnp.concatenate([top, low], axis=0))
    return out


NS = 256
OFFSET = HALF
DIAG = OFFSET + 1
PART = OFFSET + EXTRA


def flipped(matrix):
    return jnp.swapaxes(matrix, -1, -2)


def halves(value):
    high = value.astype(jnp.bfloat16)
    return high, (value - high.astype(jnp.float32)).astype(jnp.bfloat16)


def three(left, right, dims):
    lh, ll = halves(left)
    rh, rl = halves(right)

    def one(a, b):
        return lax.dot_general(a, b, (dims, ((), ())), preferred_element_type=jnp.float32)

    return one(lh, rh) + (one(lh, rl) + one(ll, rh))


def mdot(left, right):
    return three(left, right, ((1,), (0,)))


def tdot(left, right):
    return three(left, right, ((0,), (0,)))


def row_col():
    return (
        lax.broadcasted_iota(jnp.int32, (HALF, HALF), 0),
        lax.broadcasted_iota(jnp.int32, (HALF, HALF), 1),
    )


def packed(upper, corner):
    r, c = row_col()
    both = jnp.where(r >= c, upper[:, :HALF], corner)
    diag = jnp.sum(jnp.where(r == c, corner, 0.0), axis=0, keepdims=True)
    return jnp.concatenate([upper[:, HALF:], both], axis=1), diag


def unpacked(half, diag):
    r, c = row_col()
    right, both = half[:, :HALF], half[:, HALF:]
    turned = both.T
    left = jnp.where(r >= c, both, turned)
    corner = jnp.where(r < c, both, jnp.where(r == c, diag, turned))
    return jnp.concatenate(
        [jnp.concatenate([left, right], axis=1), jnp.concatenate([right.T, corner], axis=1)], axis=0
    )


def sandwich(inner, gain):
    first = mdot(inner, gain)
    upper = tdot(gain[:, :HALF], first)
    corner = tdot(gain[:, HALF:], first[:, HALF:])
    return packed(upper, corner)


def diag_row(diag):
    return jnp.concatenate([diag, jnp.zeros((1, NS - HALF), jnp.float32)], axis=1)


def store_held(out, half, diag, offset):
    out[:HALF] = half
    out[HALF:PART] = jnp.concatenate(
        [offset, diag_row(diag), jnp.zeros((EXTRA - 2, NS), jnp.float32)], axis=0
    )
    out[PART:] = jnp.zeros((NS - PART, NS), jnp.float32)


def exact(left, right, dims):
    return lax.dot_general(
        left, right, (dims, ((), ())),
        precision=lax.Precision.HIGHEST, preferred_element_type=jnp.float32,
    )


def local_kernel(
    final, mean_in, cov_in, noise_in, step_in, both, turned1, held1, mean, cov, noise, step_at, done
):
    moves = [(step_in, step_at), (cov_in.at[0], cov.at[0]), (cov_in.at[1], cov.at[1])]
    moves += [(noise_in.at[0], noise.at[0]), (noise_in.at[1], noise.at[1]), (mean_in, mean)]
    copies = [pltpu.make_async_copy(a, b, done.at[i]) for i, (a, b) in enumerate(moves)]
    for copy in copies:
        copy.start()
    copies[0].wait()
    step = step_at[...]
    moved = []
    for m in range(2):
        copies[1 + m].wait()
        moved.append(dot(step, cov[m]))
    for copy in copies[3:]:
        copy.wait()
    pred = [exact(moved[m], step, ((1,), (1,))) + noise[m] for m in range(2)]
    gains = solved_pair(pred, moved)
    gains[1] = jnp.where(final[0] == 1, 0.0, gains[1])
    means = jnp.concatenate([mean[...], jnp.zeros((EXTRA - 2, NS), jnp.float32)], axis=0)
    ahead = exact(means, step, ((1,), (1,)))
    rests = [cov[m] - exact(gains[m], moved[m], ((0,), (0,))) for m in range(2)]
    offsets = [means - dot(ahead, gains[m]) for m in range(2)]
    turned1[...] = gains[1]
    held1[:NS] = rests[1]
    held1[NS:] = jnp.broadcast_to(offsets[1][1:2], (EXTRA, NS))
    both[:NS] = mdot(gains[1], gains[0])
    both[NS : 2 * NS] = tdot(gains[0], mdot(rests[1], gains[0])) + rests[0]
    second = mdot(offsets[1], gains[0])[1:2]
    both[2 * NS :] = jnp.broadcast_to(second + offsets[0][:1], (EXTRA, NS))


def chip_kernel(core, own, other, out):
    @pl.when(core[0] == 0)
    def _():
        out[...] = mdot(other[:NS], own[:NS])

    @pl.when(core[0] == 1)
    def _():
        gain = other[:NS]
        half, diag = sandwich(own[NS : 2 * NS], gain)
        add, add_diag = packed(other[NS : NS + HALF], other[NS + HALF : 2 * NS, HALF:])
        tail = mdot(own[2 * NS :], gain) + other[2 * NS :]
        store_held(out, half + add, diag + add_diag, tail[:1])


def join_kernel(core, got, more, mine, passed, out):
    @pl.when(core[0] == 0)
    def _():
        gain = mine[...]
        out[:PART] = mdot(got[...], gain)
        out[PART:] = mdot(more[...], gain)

    @pl.when(core[0] == 1)
    def _():
        gain = passed[...]
        inner = unpacked(got[:HALF], got[DIAG : DIAG + 1, :HALF])
        half, diag = sandwich(inner, gain)
        tail = mdot(got[OFFSET:], gain)
        store_held(
            out, half + mine[:HALF], diag + mine[DIAG : DIAG + 1, :HALF],
            tail[:1] + mine[OFFSET : OFFSET + 1],
        )


def late_kernel(core, mine, passed, turned0, held0, turned1, held1, gain0, rest0, gain1, rest1):
    first = core[0] == 0
    gain = jnp.where(first, mine[...], passed[...])
    own = jnp.where(first, passed[:PART], mine[:PART])
    inner = unpacked(own[:HALF], own[HALF + 1 : HALF + 2, :HALF])
    for turned, held, full, rest in (
        (turned0[...], held0, gain0, rest0), (turned1[...], held1, gain1, rest1)
    ):
        full[...] = mdot(gain, turned)
        rest[:NS] = tdot(turned, mdot(inner, turned)) + held[:NS]
        rest[NS:] = mdot(own[HALF:], turned) + held[NS:]


def end_kernel(to_second, to_first, turned0, held0, turned1, held1, cov, mean):
    after = to_second[...] + to_first[...]
    inner = unpacked(after[:HALF], after[HALF + 1 : HALF + 2, :HALF])
    for i, (turned, held) in enumerate(((turned0, held0), (turned1, held1))):
        gain = turned[...]
        cov[i] = tdot(gain, mdot(inner, gain)) + held[:NS]
        mean[i : i + 1] = (mdot(after[HALF:], gain) + held[NS:])[:1]


def call(kernel, shapes, scalar, *arrays, far_in=False, scratch=()):
    vmem = pl.BlockSpec(memory_space=pltpu.VMEM)
    far = pl.BlockSpec(memory_space=pltpu.HBM)
    smem = pl.BlockSpec(memory_space=pltpu.SMEM)
    scalars = [] if scalar is None else [scalar]
    outs = [jax.ShapeDtypeStruct(s, jnp.float32) for s in shapes]
    done = pl.pallas_call(
        kernel,
        out_shape=outs,
        in_specs=[smem] * len(scalars) + [far if far_in else vmem] * len(arrays),
        out_specs=[vmem] * len(outs),
        scratch_shapes=scratch,
        compiler_params=pltpu.CompilerParams(vmem_limit_bytes=32 * 1024 * 1024),
    )(*scalars, *arrays)
    return done if len(outs) > 1 else done[0]


def product(left, right):
    return jnp.matmul(left, right, precision=lax.Precision.HIGHEST)


def applied(turned, held_next, held):
    width = turned.shape[0]
    first = product(held_next, turned)
    square = product(flipped(turned), first[:width]) + held[:width]
    return jnp.concatenate([square, first[width:] + held[width:]], axis=0)


def local(filt_mean, filt_cov, noise_cov, transition):
    devices = lax.axis_size(AXES)
    chips = devices // 2
    place = lax.axis_index(AXES)
    core = place % 2
    is_first = core == 0
    which = core.astype(jnp.int32)[None]
    final = (place == devices - 1).astype(jnp.int32)[None]
    wide = (NS + EXTRA, NS)
    both, turned1, held1 = call(
        local_kernel, [(2 * NS + EXTRA, NS), (NS, NS), wide], final,
        *(pltpu.with_memory_space_constraint(a, pltpu.HBM) for a in (filt_mean, filt_cov, noise_cov, transition)),
        far_in=True,
        scratch=[
            *(pltpu.VMEM(a.shape, jnp.float32) for a in (filt_mean, filt_cov, noise_cov, transition)),
            pltpu.SemaphoreType.DMA((6,)),
        ],
    )

    swap = [(p, p ^ 1) for p in range(devices)]

    def swapped(rows):
        return lax.ppermute(rows, AXES, swap)

    other = swapped(both)
    chip = call(chip_kernel, [(NS, NS)], which, both, other)
    both_turned, both_held = both[:NS], both[NS:]
    late = [jnp.where(is_first, product(other[:NS], t), t) for t in (both_turned, turned1)]
    late_held = [
        jnp.where(is_first, applied(t, other[NS:], h), h)
        for t, h in ((both_turned, both_held), (turned1, held1))
    ]

    def fetched(rows, stride, cores):
        return lax.ppermute(
            rows, AXES, [(2 * (c + stride) + k, 2 * c + k) for c in range(chips - stride) for k in cores]
        )

    def window(rows, stride):
        return fetched(rows[:PART], stride, (0, 1)), fetched(rows[PART:], stride, (0,))

    def joined(far, near):
        passed = lax.ppermute(near, AXES, [(2 * c, 2 * c + 1) for c in range(chips)])
        return call(join_kernel, [(NS, NS)], which, *far, near, passed)

    mine = fetched(chip, 1, (0, 1))
    far = fetched(chip, 2, (0, 1))
    mine = joined((far[:PART], far[PART:]), mine)
    stride = 2
    while 2 * stride < chips:
        mine = joined(window(mine, stride), mine)
        stride *= 2
    tails = mine[:PART]
    to_second, to_first = [
        lax.ppermute(tails, AXES, [(2 * (c + stride) + 1, 2 * c + k) for c in range(chips - stride)])
        for k in (1, 0)
    ]
    passed = swapped(mine)
    square = (NS, NS)
    gain0, rest0, gain1, rest1 = call(
        late_kernel, [square, wide, square, wide], which, mine, passed,
        late[0], late_held[0], late[1], late_held[1],
    )
    smooth_cov, smooth_mean = call(
        end_kernel, [(2, NS, NS), (2, NS)], None, to_second, to_first, gain0, rest0, gain1, rest1
    )
    return (smooth_mean, smooth_cov)


def solution(mesh):
    in_specs = (P(AXES, None), P(AXES, None, None), P(AXES, None, None), P())
    out_specs = (P(AXES, None), P(AXES, None, None))
    return jax.shard_map(local, mesh=mesh, in_specs=in_specs, out_specs=out_specs, check_vma=False)
```

```python
import jax
import jax.numpy as jnp
from jax import lax
from jax.experimental import pallas as pl
from jax.experimental.pallas import tpu as pltpu
from jax.sharding import PartitionSpec as P

AXES = ("grp", "dev")
EXTRA = 8

BASE = 16
HALF = 128


def dot(left, right):
    return jnp.dot(left, right, precision=lax.Precision.HIGHEST, preferred_element_type=jnp.float32)


def eliminated(tops, base):
    tiles = [[t[8 * i : 8 * i + 8] for i in range(BASE // 8)] for t in tops]
    lane = lax.broadcasted_iota(jnp.int32, (8, HALF), 1)
    sub = lax.broadcasted_iota(jnp.int32, (8, HALF), 0)

    def spread(row):
        return jnp.broadcast_to(row, (8, HALF))

    cols = [[[spread(t[:, base + j : base + j + 1]) for t in tiles[m]] for j in range(BASE)] for m in range(2)]
    for k in range(BASE):
        q, o = divmod(k, 8)
        here = lane == base + k
        unit = jnp.where(sub == o, 1.0, 0.0)
        for m in range(2):
            col, tile = cols[m], tiles[m]
            ratio = 1.0 / spread(col[k][q][o : o + 1])
            scaled = jnp.where(here, ratio, spread(tile[q][o : o + 1]) * ratio)
            down = list(col[k])
            down[q] = down[q] - unit
            for j in range(k + 1, BASE):
                f = spread(col[j][q][o : o + 1]) * ratio
                col[j] = [c - d * f for c, d in zip(col[j], down)]
            for i in range(BASE // 8):
                old = jnp.where(here, unit if i == q else 0.0, tile[i])
                tile[i] = old - down[i] * scaled
    return [jnp.concatenate(t, axis=0) for t in tiles]


def less_product(rows, base, inside, new):
    parts = []
    for i in range(BASE // 8):
        old = rows[8 * i : 8 * i + 8]
        terms = [
            jnp.broadcast_to(old[:, base + k : base + k + 1], (8, HALF)) * jnp.broadcast_to(new[k : k + 1], (8, HALF))
            for k in range(BASE)
        ]
        while len(terms) > 1:
            terms = [a + b for a, b in zip(terms[::2], terms[1::2])]
        parts.append(jnp.where(inside[:8], 0.0, old) - terms[0])
    return jnp.concatenate(parts, axis=0)


def half_inverse(pair):
    lane = lax.broadcasted_iota(jnp.int32, (BASE, HALF), 1)
    count = HALF // BASE
    pair = [[p[BASE * i : BASE * i + BASE] for i in range(count)] for p in pair]
    for j in range(count):
        rows = slice(BASE * j, BASE * j + BASE)
        inside = (lane >= BASE * j) & (lane < BASE * (j + 1))
        news = eliminated([p[j] for p in pair], BASE * j)
        for m in range(2):
            first = (j + 1) % count
            rest = [i for i in range(count) if i not in (j, first)]
            old = pair[m]
            new = [None] * count
            new[j] = news[m]
            new[first] = less_product(old[first], BASE * j, inside, news[m])
            tall = jnp.concatenate([old[i][:, rows] for i in rest], axis=0)
            tall = dot(tall, news[m])
            for n, i in enumerate(rest):
                new[i] = jnp.where(inside, 0.0, old[i]) - tall[BASE * n : BASE * n + BASE]
            pair[m] = new
    return [jnp.concatenate(p, axis=0) for p in pair]


def solved_pair(pred, moved):
    lo, hi = slice(0, HALF), slice(HALF, 2 * HALF)
    inv = half_inverse([p[lo, lo] for p in pred])
    wide, corner, out = [], [], []
    for m in range(2):
        wide.append(dot(inv[m], jnp.concatenate([pred[m][lo, hi], moved[m][lo]], axis=1)))
        corner.append(pred[m][hi, hi] - dot(pred[m][hi, lo], wide[m][:, :HALF]))
    inv = half_inverse(corner)
    for m in range(2):
        rest = moved[m][hi] - dot(pred[m][hi, lo], wide[m][:, HALF:])
        low = dot(inv[m], rest)
        top = wide[m][:, HALF:] - dot(wide[m][:, :HALF], low)
        out.append(jnp.concatenate([top, low], axis=0))
    return out


NS = 256
TOP = 192
LOW = NS - TOP
OFFSET = LOW + HALF
DIAG = OFFSET + 1
PART = OFFSET + EXTRA


def flipped(matrix):
    return jnp.swapaxes(matrix, -1, -2)


def halves(value):
    high = value.astype(jnp.bfloat16)
    return high, (value - high.astype(jnp.float32)).astype(jnp.bfloat16)


def three(left, right, dims):
    lh, ll = halves(left)
    rh, rl = halves(right)

    def one(a, b):
        return lax.dot_general(a, b, (dims, ((), ())), preferred_element_type=jnp.float32)

    return one(lh, rh) + (one(lh, rl) + one(ll, rh))


def mdot(left, right):
    return three(left, right, ((1,), (0,)))


def tdot(left, right):
    return three(left, right, ((0,), (0,)))


def row_col():
    return (
        lax.broadcasted_iota(jnp.int32, (HALF, HALF), 0),
        lax.broadcasted_iota(jnp.int32, (HALF, HALF), 1),
    )


def packed(upper, corner):
    r, c = row_col()
    both = jnp.where(r >= c, upper[:, :HALF], corner)
    diag = jnp.sum(jnp.where(r == c, corner, 0.0), axis=0, keepdims=True)
    return jnp.concatenate([upper[:, HALF:], both], axis=1), diag


def unpacked(half, diag):
    r, c = row_col()
    right, both = half[:, :HALF], half[:, HALF:]
    turned = both.T
    left = jnp.where(r >= c, both, turned)
    corner = jnp.where(r < c, both, jnp.where(r == c, diag, turned))
    return jnp.concatenate(
        [jnp.concatenate([left, right], axis=1), jnp.concatenate([right.T, corner], axis=1)], axis=0
    )


def sandwich(inner, gain):
    first = mdot(inner, gain)
    upper = tdot(gain[:, :HALF], first)
    corner = tdot(gain[:, HALF:], first[:, HALF:])
    return packed(upper, corner)


def diag_row(diag):
    return jnp.concatenate([diag, jnp.zeros((1, NS - HALF), jnp.float32)], axis=1)


def store_held(out, base, half, diag, offset):
    out[base : base + HALF] = half
    tail = jnp.concatenate(
        [offset, diag_row(diag), jnp.zeros((EXTRA - 2, NS), jnp.float32)], axis=0
    )
    out[base + HALF : base + HALF + EXTRA] = tail


def exact(left, right, dims):
    return lax.dot_general(
        left, right, (dims, ((), ())),
        precision=lax.Precision.HIGHEST, preferred_element_type=jnp.float32,
    )


def local_kernel(
    final, mean_in, cov_in, noise_in, step_in, both, turned1, held1, mean, cov, noise, step_at, done
):
    moves = [(step_in, step_at), (cov_in.at[0], cov.at[0]), (cov_in.at[1], cov.at[1])]
    moves += [(noise_in.at[0], noise.at[0]), (noise_in.at[1], noise.at[1]), (mean_in, mean)]
    copies = [pltpu.make_async_copy(a, b, done.at[i]) for i, (a, b) in enumerate(moves)]
    for copy in copies:
        copy.start()
    copies[0].wait()
    step = step_at[...]
    moved = []
    for m in range(2):
        copies[1 + m].wait()
        moved.append(dot(step, cov[m]))
    for copy in copies[3:]:
        copy.wait()
    pred = [exact(moved[m], step, ((1,), (1,))) + noise[m] for m in range(2)]
    gains = solved_pair(pred, moved)
    gains[1] = jnp.where(final[0] == 1, 0.0, gains[1])
    means = jnp.concatenate([mean[...], jnp.zeros((EXTRA - 2, NS), jnp.float32)], axis=0)
    ahead = exact(means, step, ((1,), (1,)))
    rests = [cov[m] - exact(gains[m], moved[m], ((0,), (0,))) for m in range(2)]
    offsets = [means - dot(ahead, gains[m]) for m in range(2)]
    turned1[...] = gains[1]
    held1[:NS] = rests[1]
    held1[NS:] = jnp.broadcast_to(offsets[1][1:2], (EXTRA, NS))
    both[:NS] = mdot(gains[1], gains[0])
    both[NS : 2 * NS] = tdot(gains[0], mdot(rests[1], gains[0])) + rests[0]
    second = mdot(offsets[1], gains[0])[1:2]
    both[2 * NS :] = jnp.broadcast_to(second + offsets[0][:1], (EXTRA, NS))


def chip_kernel(core, own, other, out):
    @pl.when(core[0] == 0)
    def _():
        out[:TOP] = mdot(other[:TOP], own[:NS])
        out[TOP:] = jnp.zeros((PART - TOP, NS), jnp.float32)

    @pl.when(core[0] == 1)
    def _():
        gain = other[:NS]
        out[:LOW] = mdot(own[TOP:NS], gain)
        half, diag = sandwich(own[NS : 2 * NS], gain)
        add, add_diag = packed(other[NS : NS + HALF], other[NS + HALF : 2 * NS, HALF:])
        tail = mdot(own[2 * NS :], gain) + other[2 * NS :]
        store_held(out, LOW, half + add, diag + add_diag, tail[:1])


def join_kernel(core, got, mine, passed, out):
    @pl.when(core[0] == 0)
    def _():
        gain = jnp.concatenate([mine[:TOP], passed[:LOW]], axis=0)
        out[:TOP] = mdot(got[:TOP], gain)
        out[TOP:] = jnp.zeros((PART - TOP, NS), jnp.float32)

    @pl.when(core[0] == 1)
    def _():
        gain = jnp.concatenate([passed[:TOP], mine[:LOW]], axis=0)
        out[:LOW] = mdot(got[:LOW], gain)
        inner = unpacked(got[LOW:OFFSET], got[DIAG : DIAG + 1, :HALF])
        half, diag = sandwich(inner, gain)
        tail = mdot(got[OFFSET:], gain)
        store_held(
            out, LOW, half + mine[LOW:OFFSET], diag + mine[DIAG : DIAG + 1, :HALF],
            tail[:1] + mine[OFFSET : OFFSET + 1],
        )


def late_kernel(core, mine, passed, turned0, held0, turned1, held1, gain0, rest0, gain1, rest1):
    first = core[0] == 0
    gain = jnp.where(
        first,
        jnp.concatenate([mine[:TOP], passed[:LOW]], axis=0),
        jnp.concatenate([passed[:TOP], mine[:LOW]], axis=0),
    )
    own = jnp.where(first, passed[LOW:], mine[LOW:])
    inner = unpacked(own[:HALF], own[HALF + 1 : HALF + 2, :HALF])
    for turned, held, full, rest in (
        (turned0[...], held0, gain0, rest0), (turned1[...], held1, gain1, rest1)
    ):
        full[...] = mdot(gain, turned)
        rest[:NS] = tdot(turned, mdot(inner, turned)) + held[:NS]
        rest[NS:] = mdot(own[HALF:], turned) + held[NS:]


def end_kernel(to_second, to_first, turned0, held0, turned1, held1, cov, mean):
    after = to_second[...] + to_first[...]
    inner = unpacked(after[:HALF], after[HALF + 1 : HALF + 2, :HALF])
    for i, (turned, held) in enumerate(((turned0, held0), (turned1, held1))):
        gain = turned[...]
        cov[i] = tdot(gain, mdot(inner, gain)) + held[:NS]
        mean[i : i + 1] = (mdot(after[HALF:], gain) + held[NS:])[:1]


def call(kernel, shapes, scalar, *arrays, far_in=False, scratch=()):
    vmem = pl.BlockSpec(memory_space=pltpu.VMEM)
    far = pl.BlockSpec(memory_space=pltpu.HBM)
    smem = pl.BlockSpec(memory_space=pltpu.SMEM)
    scalars = [] if scalar is None else [scalar]
    outs = [jax.ShapeDtypeStruct(s, jnp.float32) for s in shapes]
    done = pl.pallas_call(
        kernel,
        out_shape=outs,
        in_specs=[smem] * len(scalars) + [far if far_in else vmem] * len(arrays),
        out_specs=[vmem] * len(outs),
        scratch_shapes=scratch,
        compiler_params=pltpu.CompilerParams(vmem_limit_bytes=32 * 1024 * 1024),
    )(*scalars, *arrays)
    return done if len(outs) > 1 else done[0]


def product(left, right):
    return jnp.matmul(left, right, precision=lax.Precision.HIGHEST)


def applied(turned, held_next, held):
    width = turned.shape[0]
    first = product(held_next, turned)
    square = product(flipped(turned), first[:width]) + held[:width]
    return jnp.concatenate([square, first[width:] + held[width:]], axis=0)


def local(filt_mean, filt_cov, noise_cov, transition):
    devices = lax.axis_size(AXES)
    chips = devices // 2
    place = lax.axis_index(AXES)
    core = place % 2
    is_first = core == 0
    which = core.astype(jnp.int32)[None]
    final = (place == devices - 1).astype(jnp.int32)[None]
    wide = (NS + EXTRA, NS)
    both, turned1, held1 = call(
        local_kernel, [(2 * NS + EXTRA, NS), (NS, NS), wide], final,
        *(pltpu.with_memory_space_constraint(a, pltpu.HBM) for a in (filt_mean, filt_cov, noise_cov, transition)),
        far_in=True,
        scratch=[
            *(pltpu.VMEM(a.shape, jnp.float32) for a in (filt_mean, filt_cov, noise_cov, transition)),
            pltpu.SemaphoreType.DMA((6,)),
        ],
    )

    swap = [(p, p ^ 1) for p in range(devices)]

    def swapped(rows):
        return lax.ppermute(rows, AXES, swap)

    other = swapped(both)
    chip = call(chip_kernel, [(PART, NS)], which, both, other)
    both_turned, both_held = both[:NS], both[NS:]
    late = [jnp.where(is_first, product(other[:NS], t), t) for t in (both_turned, turned1)]
    late_held = [
        jnp.where(is_first, applied(t, other[NS:], h), h)
        for t, h in ((both_turned, both_held), (turned1, held1))
    ]

    def fetched(rows, stride, cores):
        return lax.ppermute(
            rows, AXES, [(2 * (c + stride) + k, 2 * c + k) for c in range(chips - stride) for k in cores]
        )

    mine = fetched(chip, 1, (0, 1))
    got = fetched(chip, 2, (0, 1))
    stride = 2
    passed = swapped(mine[:TOP])
    mine = call(join_kernel, [(PART, NS)], which, got, mine, passed)
    while 2 * stride < chips:
        pairs = [(2 * (c + stride) + 1, 2 * c + 1) for c in range(chips - stride)]
        pairs += [(2 * (c + stride), 2 * c) for c in range(chips - 2 * stride)]
        got = lax.ppermute(mine, AXES, pairs)
        passed = swapped(mine[:TOP])
        mine = call(join_kernel, [(PART, NS)], which, got, mine, passed)
        stride *= 2
    tails = mine[LOW:]
    to_second, to_first = [
        lax.ppermute(tails, AXES, [(2 * (c + stride) + 1, 2 * c + k) for c in range(chips - stride)])
        for k in (1, 0)
    ]
    passed = swapped(mine)
    square = (NS, NS)
    gain0, rest0, gain1, rest1 = call(
        late_kernel, [square, wide, square, wide], which, mine, passed,
        late[0], late_held[0], late[1], late_held[1],
    )
    smooth_cov, smooth_mean = call(
        end_kernel, [(2, NS, NS), (2, NS)], None, to_second, to_first, gain0, rest0, gain1, rest1
    )
    return (smooth_mean, smooth_cov)


def solution(mesh):
    in_specs = (P(AXES, None), P(AXES, None, None), P(AXES, None, None), P())
    out_specs = (P(AXES, None), P(AXES, None, None))
    return jax.shard_map(local, mesh=mesh, in_specs=in_specs, out_specs=out_specs, check_vma=False)
```
